256 devices in a mesh: tm: 32 (over z, y_lo, core), space: 8 (over x, y_hi).
Axes of the slice: x: 4, y: 4 (y_hi: 2, y_lo: 2; y = y_hi * 2 + y_lo), z: 8, core: 2. Of those that a mesh axis runs over, the one named last changes fastest.
Arguments:
- flux_solution_stack: float32 [128, 1024, 1024], P('tm', 'space'), may hold values from -6 to 6
- source: float32 [128, 1024, 1024], P('tm', 'space'), may hold values from -6 to 6
- notch_offsets: int32 [128], P('tm'), may hold values from 0 to 127
- region_ids: int32 [1024, 1024], P('space'), may hold values from 0 to 7
- nu_table: float32 [8], replicated, may hold values from 0.1 to 10
- sigma_table: float32 [8], replicated, may hold values from 0.05 to 1
Outputs:
- updated: float32 [128, 1024, 1024], P('tm', 'space')
- correction: float32 [1024, 1024], P('space')
The draws below stay inside these ranges and needn't reach their ends.
All inputs are finite; a program needn't handle non-finite values.
Results may differ from the reference program's by a relative error of at most 0.0003.
Values sent between devices are 32-bit elements; how exact they have to be, the bound alone decides.
No kernel may reach another device: no remote copies, remote signals or barrier semaphores. Data moves between devices by JAX's collectives and lax.ppermute only.
A program may use at most 64 MiB of HBM per device.

```python
import math
import jax
import jax.numpy as jnp
from jax import lax

ARC_CELL_COUNT = 1024
SLOT_W = 8
REGIONS = 8
SWEEPS = 4
CYCLE_MOMENTS = 128
RADIAL_COUNT = 1024
ROTOR_ROWS = 512
ROTOR_NOTCHES = 128


def draw_source(key, part):
    key = jax.random.fold_in(key, 11)
    perturbation_seed, phase_random_key = jax.random.split(key, 2)
    moment_indices = jnp.arange(CYCLE_MOMENTS, dtype=jnp.int32)
    alternating_factors = jnp.where(moment_indices < CYCLE_MOMENTS // 2, 1.0, -1.0).astype(jnp.float32)
    radial_pos = (jnp.arange(RADIAL_COUNT, dtype=jnp.float32) + 0.5) / RADIAL_COUNT
    angle_pos = jnp.arange(ARC_CELL_COUNT, dtype=jnp.float32) / ARC_CELL_COUNT
    phase_shift = jax.random.uniform(phase_random_key, (), jnp.float32, 0.0, 2.0 * jnp.pi)
    perturbation_term = jax.random.normal(perturbation_seed, (CYCLE_MOMENTS, RADIAL_COUNT, ARC_CELL_COUNT), jnp.float32)
    amplitude = 2.0
    wave_count = 2.0
    angular_shape = 1.0 + 0.5 * jnp.cos(2.0 * jnp.pi * wave_count * angle_pos + phase_shift)
    radial_shape = jnp.sin(jnp.pi * radial_pos)
    smooth_part = amplitude * radial_shape[:, None] * angular_shape[None, :]
    return jnp.clip(perturbation_term + alternating_factors[:, None, None] * smooth_part[None], -6.0, 6.0)


def plant(values, key, smallest, largest):
    index_at = [jax.random.randint(jax.random.fold_in(key, axis), (), 0, length) for axis, length in enumerate(values.shape)]
    widest = values.shape.index(max(values.shape))
    beside = index_at[:widest] + [(index_at[widest] + 1) % values.shape[widest]] + index_at[widest + 1:]
    return values.at[tuple(index_at)].set(smallest).at[tuple(beside)].set(largest)


def steps_of(own_key, shape, cuts, smallest, top_value):
    gain, own = 1.0, jax.random.fold_in(own_key, 6)
    for position, parts in cuts:
        heights = jnp.exp(jax.random.uniform(jax.random.fold_in(own, position), (parts,), jnp.float32, smallest / len(cuts), top_value / len(cuts)))
        gain = gain * jnp.repeat(heights, shape[position] // parts).reshape([-1 if axis == position else 1 for axis in range(len(shape))])
    return gain


def centred(own_key, dims, width, limit, cuts=(), kind=jnp.bfloat16):
    array = jax.random.normal(own_key, dims, jnp.float32) * width
    if len(cuts) > 0:
        array = steps_of(own_key, dims, cuts, -0.22, 0.18) * array
    return jnp.clip(array, min=-limit, max=limit).astype(kind)


def setup_inputs(seed: int = 0) -> dict:
    streams_of = jax.random.split(jax.random.key(seed), 7)
    flux_solution_stack = centred(streams_of[0], (CYCLE_MOMENTS, RADIAL_COUNT, ARC_CELL_COUNT), 1.0, 6.0, ((0, 32), (1, 8)), jnp.float32)
    source = draw_source(jax.random.fold_in(streams_of[6], 71), 0)
    notch_offsets = plant(jax.random.randint(streams_of[2], (CYCLE_MOMENTS,), 0, ROTOR_NOTCHES), jax.random.fold_in(streams_of[2], 1), 0, ROTOR_NOTCHES - 1).astype(jnp.int32)
    region_ids = plant(jax.random.randint(streams_of[3], (RADIAL_COUNT, ARC_CELL_COUNT), 0, REGIONS), jax.random.fold_in(streams_of[3], 1), 0, REGIONS - 1).astype(jnp.int32)
    nu_table = jnp.clip(jnp.exp(jax.random.uniform(streams_of[4], (REGIONS,), jnp.float32, math.log(0.1), math.log(10.0))), 0.1, 10.0)
    sigma_table = jnp.clip(jnp.exp(jax.random.uniform(streams_of[5], (REGIONS,), jnp.float32, math.log(0.05), math.log(1.0))), 0.05, 1.0)
    return dict(flux_solution_stack=flux_solution_stack, source=source, notch_offsets=notch_offsets, region_ids=region_ids, nu_table=nu_table, sigma_table=sigma_table)


minimum_floor = 0.2
upper_limit = 2.0


def lookup(region_map, table):
    result = jnp.zeros(region_map.shape, jnp.float32)
    for region in range(REGIONS):
        result = result + jnp.where(region_map == region, table[region], jnp.float32(0.0))
    return result


def harmonic(left, right):
    return 2.0 * left * right / (left + right)


def material_kinds(ids_pad, shift, rotor, nu_table, sigma_table):
    moved = jnp.where(rotor, jnp.roll(ids_pad, shift * SLOT_W, axis=1), ids_pad)
    nu_pad = lookup(moved, nu_table)
    sigma_cells = lookup(moved[1:-1], sigma_table)
    facet_lines = harmonic(nu_pad[:-1], nu_pad[1:])
    core = nu_pad[1:-1]
    wrapped = jnp.concatenate([core[:, -1:], core, core[:, :1]], axis=1)
    face_cols = harmonic(wrapped[:, :-1], wrapped[:, 1:])
    return facet_lines, face_cols, sigma_cells


def wrap_cols(field):
    return jnp.concatenate([field[:, -1:], field, field[:, :1]], axis=1)


def operate(field, row_pad, col_pad, facet_lines, face_cols, sigma_cells):
    result = sigma_cells * field
    result = result + facet_lines[:-1] * (field - row_pad[:-2]) + facet_lines[1:] * (field - row_pad[2:])
    result = result + face_cols[:, :-1] * (field - col_pad[:, :-2]) + face_cols[:, 1:] * (field - col_pad[:, 2:])
    return result


def diagonal_of(facet_lines, face_cols, sigma_cells):
    return sigma_cells + facet_lines[:-1] + facet_lines[1:] + face_cols[:, :-1] + face_cols[:, 1:]


def chebyshev(desired_result, apply_op, diagonal):
    center = (upper_limit + minimum_floor) / 2.0
    half_span_width = (upper_limit - minimum_floor) / 2.0
    ratio = center / half_span_width
    coef_old = 1.0 / ratio
    resid = desired_result
    step_field = resid / diagonal / center
    corr = step_field
    for sweep in range(SWEEPS - 1):
        resid = resid - apply_op(step_field)
        coef_new = 1.0 / (2.0 * ratio - coef_old)
        step_field = coef_new * coef_old * step_field + (2.0 * coef_new / half_span_width) * (resid / diagonal)
        corr = corr + step_field
        coef_old = coef_new
    return corr


def reference(flux_solution_stack, source, notch_offsets, region_ids, nu_table, sigma_table):
    ids_pad = jnp.pad(region_ids, ((1, 1), (0, 0)))
    global_rows = jnp.arange(-1, RADIAL_COUNT + 1, dtype=jnp.int32)
    rotor = (global_rows < ROTOR_ROWS)[:, None]
    polarity_factors = jnp.where(jnp.arange(CYCLE_MOMENTS) < CYCLE_MOMENTS // 2, 1.0, -1.0).astype(jnp.float32)

    def accumulate(combined_accumulation, items):
        field, current, shift, sign = items
        facet_lines, face_cols, sigma_cells = material_kinds(ids_pad, shift, rotor, nu_table, sigma_table)
        row_pad = jnp.pad(field, ((1, 1), (0, 0)))
        image = operate(field, row_pad, wrap_cols(field), facet_lines, face_cols, sigma_cells)
        return combined_accumulation + sign * (current - image), None

    combined_accumulation, _ = lax.scan(accumulate, jnp.zeros((RADIAL_COUNT, ARC_CELL_COUNT), jnp.float32), (flux_solution_stack, source, notch_offsets, polarity_factors))
    desired_result = combined_accumulation / CYCLE_MOMENTS
    facet_lines, face_cols, sigma_cells = material_kinds(ids_pad, jnp.int32(0), rotor, nu_table, sigma_table)
    diagonal = diagonal_of(facet_lines, face_cols, sigma_cells)

    def apply_op(field):
        return operate(field, jnp.pad(field, ((1, 1), (0, 0))), wrap_cols(field), facet_lines, face_cols, sigma_cells)

    corr = chebyshev(desired_result, apply_op, diagonal)
    image = apply_op(corr)
    omega = jnp.sum(desired_result * corr) / jnp.sum(corr * image)
    correction = omega * corr
    opposite_moment_potential = jnp.roll(flux_solution_stack, CYCLE_MOMENTS // 2, axis=0)
    updated = flux_solution_stack - 0.5 * (flux_solution_stack + opposite_moment_potential) + polarity_factors[:, None, None] * correction[None]
    return updated, correction
```

```python
import functools

import jax
import jax.numpy as jnp
from jax import lax
from jax.experimental import pallas as pl
from jax.experimental.pallas import tpu as pltpu
from jax.sharding import PartitionSpec as P

SLOT_W = 8
REGIONS = 8
SWEEPS = 4
MINIMUM = 0.2
MAXIMUM = 2.0
ROWS = 128
COLS = 1024
STEPS = 4
PADDED = ROWS + 32
FIRST = 16
EARLY = 48
TILE = 16

ANY = pl.BlockSpec(memory_space=pl.ANY)
VMEM = pl.BlockSpec(memory_space=pltpu.VMEM)
SMEM = pl.BlockSpec(memory_space=pltpu.SMEM)
LIMIT = pltpu.CompilerParams(vmem_limit_bytes=16 * 1024 * 1024)


def struct(*shape):
    return jax.ShapeDtypeStruct(shape, jnp.float32)


def block(i):
    return pl.ds(pl.multiple_of(i * 8, 8), 8)


def harmonic(left, right):
    return 2.0 * left * right / (left + right)


def above(cur, prev, first):
    return jnp.where(first, pltpu.roll(prev, 1, 0), pltpu.roll(cur, 1, 0))


def below(cur, after, last):
    return jnp.where(last, pltpu.roll(after, 7, 0), pltpu.roll(cur, 7, 0))


def row_masks():
    rows = lax.broadcasted_iota(jnp.int32, (8, COLS), 0)
    return rows == 0, rows == 7


def edges_kernel(first_p, last_p, first_ids, last_ids, down_ref, up_ref):
    for out, p, ids, row in ((down_ref, first_p, first_ids, 0), (up_ref, last_p, last_ids, 7)):
        for k in range(STEPS):
            out[k : k + 1, :] = p[k, row : row + 1, :]
            out[STEPS + k : STEPS + k + 1, :] = p[k, row : row + 1, :]
        out[8:16, :] = ids[...].astype(jnp.float32)


def edges(p, ids):
    tail = ROWS // 8 - 1
    return pl.pallas_call(
        edges_kernel,
        grid=(1,),
        in_specs=[
            pl.BlockSpec((STEPS, 8, COLS), lambda i: (0, 0, 0)),
            pl.BlockSpec((STEPS, 8, COLS), lambda i: (0, tail, 0)),
            pl.BlockSpec((8, COLS), lambda i: (0, 0)),
            pl.BlockSpec((8, COLS), lambda i: (tail, 0)),
        ],
        out_specs=[pl.BlockSpec((16, COLS), lambda i: (0, 0))] * 2,
        out_shape=[struct(16, COLS)] * 2,
    )(p, p, ids, ids)


def residual_kernel(
    offs, nu_t, sg_t, p, src, ids, top, bot, mine, send, sg, fr, fc, nu, v, fr_k
):
    first, last = row_masks()
    strip, tm = lax.axis_index("space"), lax.axis_index("tm")
    half_strips = lax.axis_size("space") // 2

    def materials(where, region):
        n = jnp.full((8, COLS), nu_t[0], jnp.float32)
        s = jnp.full((8, COLS), sg_t[0], jnp.float32)
        for r in range(1, REGIONS):
            hit = region == r
            n = jnp.where(hit, nu_t[r], n)
            s = jnp.where(hit, sg_t[r], s)
        nu[where, :] = n
        sg[where, :] = s

    materials(pl.ds(8, 8), top[8:16, :].astype(jnp.int32))
    materials(pl.ds(FIRST + ROWS, 8), bot[8:16, :].astype(jnp.int32))

    @pl.loop(0, ROWS // 8)
    def _(b):
        materials(block(b + 2), ids[block(b), :])

    zeros = jnp.zeros((8, COLS), jnp.float32)
    for ref in (sg, fr, fc):
        ref[0:8, :] = zeros
        ref[PADDED - 8 : PADDED, :] = zeros
    nu[0:8, :] = nu[8:16, :]
    nu[PADDED - 8 : PADDED, :] = nu[PADDED - 16 : PADDED - 8, :]

    @pl.loop(1, PADDED // 8 - 1)
    def _(b):
        cur = nu[block(b), :]
        face = harmonic(cur, below(cur, nu[block(b + 1), :], last))
        fr[block(b), :] = face
        fr_k[block(b), :] = face
        fc[block(b), :] = harmonic(cur, pltpu.roll(cur, COLS - 1, 1))

    sign = jnp.where(tm < lax.axis_size("tm") // 2, 1.0, -1.0).astype(jnp.float32)
    scale = sign / (STEPS * lax.axis_size("tm"))
    core, y = tm & 1, (tm >> 1) & 1
    flip = core * 8 + y * 4

    for k in range(STEPS):
        turn = offs[k] * SLOT_W
        own = jnp.where(strip < half_strips, turn, 0)
        for halo, at, kind, face_row in (
            (top, slice(15, 16), strip - 1, FIRST - 1),
            (bot, slice(FIRST + ROWS, FIRST + ROWS + 1), strip + 1, FIRST + ROWS - 1),
        ):
            other = jnp.where(kind < half_strips, turn, 0)
            beside = jnp.broadcast_to(nu[at, :], (8, COLS))
            beside = pltpu.roll(beside, (other - own) & (COLS - 1), 1)
            edge = FIRST if halo is top else FIRST + ROWS - 1
            face = harmonic(beside, jnp.broadcast_to(nu[edge : edge + 1, :], (8, COLS)))
            fr_k[face_row : face_row + 1, :] = face[0:1, :]
            row = jnp.broadcast_to(halo[k : k + 1, :], (8, COLS))
            row = pltpu.roll(row, (-own) & (COLS - 1), 1)
            if halo is top:
                v[8:16, :] = row
            else:
                v[FIRST + ROWS : FIRST + ROWS + 8, :] = row

        @pl.loop(0, ROWS // 8, unroll=2)
        def _(b):
            v[block(b + 2), :] = pltpu.roll(p[k, block(b), :], (-own) & (COLS - 1), 1)

        for out, shift in ((mine, 0), (send, 8)):

            @pl.loop(0, ROWS // 16, unroll=2)
            def _(i):
                b = (i + shift) ^ flip
                e = b + 2
                cur = v[block(e), :]
                down_face = fr_k[block(e), :]
                up_face = above(down_face, fr_k[block(e - 1), :], first)
                image = sg[block(e), :] * cur
                image += up_face * (cur - above(cur, v[block(e - 1), :], first))
                image += down_face * (cur - below(cur, v[block(e + 1), :], last))
                flow = fc[block(e), :] * (cur - pltpu.roll(cur, COLS - 1, 1))
                image += flow - pltpu.roll(flow, 1, 1)
                part = scale * (src[k, block(b), :] - pltpu.roll(image, own, 1))
                out[block(i), :] = part if k == 0 else out[block(i), :] + part


def residual(offs, nu_t, sg_t, p, src, ids, top, bot):
    return pl.pallas_call(
        residual_kernel,
        in_specs=[SMEM] * 3 + [VMEM] * 5,
        out_specs=[VMEM] * 5,
        out_shape=[struct(ROWS // 2, COLS)] * 2 + [struct(PADDED, COLS)] * 3,
        scratch_shapes=[pltpu.VMEM((PADDED, COLS), jnp.float32)] * 3,
        compiler_params=LIMIT,
        cost_estimate=pl.CostEstimate(flops=20_000_000, bytes_accessed=8_000_000, transcendentals=0),
    )(offs, nu_t, sg_t, p, src, ids, top, bot)


def swap(x, bit):
    return lax.ppermute(x, "tm", [(i, i ^ bit) for i in range(lax.axis_size("tm"))])


def add_kernel(a, b, mine, send):
    n = mine.shape[0]
    mine[...] = a[:n, :] + b[:n, :]
    send[...] = a[n:, :] + b[n:, :]


def halves(a, b):
    n = a.shape[0] // 2
    return pl.pallas_call(
        add_kernel,
        in_specs=[VMEM] * 2,
        out_specs=[VMEM] * 2,
        out_shape=[struct(n, COLS)] * 2,
    )(a, b)


def merge_kernel(a, b, _, out):
    for z in range(out.shape[0]):
        piece = slice(z * 128, z * 128 + 128)
        out[z] = a[:, piece] + b[:, piece]


def merge(a, b, after, count):
    return pl.pallas_call(
        merge_kernel,
        in_specs=[VMEM, VMEM, ANY],
        out_specs=VMEM,
        out_shape=struct(count, a.shape[0], COLS // count),
    )(a, b, after)


def total_kernel(parts, out):
    total = parts[0]
    for i in range(1, parts.shape[0]):
        total = total + parts[i]
    for i in range(parts.shape[0]):
        out[i] = total


def total_for_all(parts):
    return pl.pallas_call(
        total_kernel,
        in_specs=[VMEM],
        out_specs=VMEM,
        out_shape=struct(*parts.shape),
    )(parts)


def among_z(blocks):
    groups = [[z * 4 + q for z in range(blocks.shape[0])] for q in range(4)]
    return lax.all_to_all(blocks, "tm", 0, 0, axis_index_groups=groups)


def gate_kernel(value, _, out):
    pass


def gate(value, after):
    return pl.pallas_call(
        gate_kernel,
        in_specs=[ANY, ANY],
        out_specs=ANY,
        out_shape=struct(*value.shape),
        input_output_aliases={0: 0},
    )(value, after)


def assemble_kernel(x, other, core_part, target, top, bot):
    tm = lax.axis_index("tm")
    flip = (tm & 1) * 8 + ((tm >> 1) & 1) * 4
    count = x.shape[0]
    for ref, lead, start in ((x, 0, 0), (other, 0, 4), (core_part, 0, 8), (core_part, count, 12)):
        for i in range(4):
            for z in range(count):
                piece = slice(z * 128, z * 128 + 128)
                target[block((start + i) ^ flip), piece] = ref[lead + z, 8 * i : 8 * i + 8, :]
    top[...] = target[0:8, :]
    bot[...] = target[ROWS - 8 : ROWS, :]


def assemble(x, other, core_part):
    return pl.pallas_call(
        assemble_kernel,
        in_specs=[VMEM] * 3,
        out_specs=[VMEM] * 3,
        out_shape=[struct(ROWS, COLS), struct(8, COLS), struct(8, COLS)],
    )(x, other, core_part)


def chebyshev_kernel(target, top, bot, sg, fr, fc, c_out, sums, dinv, res, s0, s1, c):
    first, last = row_masks()
    strip = lax.axis_index("space")
    blocks = PADDED // 8
    zeros = jnp.zeros((8, COLS), jnp.float32)
    for ref in (s0, s1, c, dinv):
        ref[0:8, :] = zeros
        ref[PADDED - 8 : PADDED, :] = zeros
    res[8:16, :] = top[...]
    res[FIRST + ROWS : FIRST + ROWS + 8, :] = bot[...]
    res[FIRST : FIRST + ROWS, :] = target[...]

    center = (MAXIMUM + MINIMUM) / 2.0
    half_span = (MAXIMUM - MINIMUM) / 2.0
    ratio = center / half_span

    @pl.loop(1, blocks - 1)
    def _(e):
        down_face, cell = fr[block(e), :], fc[block(e), :]
        diagonal = (
            sg[block(e), :]
            + above(down_face, fr[block(e - 1), :], first)
            + down_face
            + pltpu.roll(cell, 1, 1)
            + cell
        )
        outside = ((strip == 0) & (e == 1)) | (
            (strip == lax.axis_size("space") - 1) & (e == blocks - 2)
        )
        inverse = jnp.where(outside, 0.0, 1.0 / diagonal)
        dinv[block(e), :] = inverse
        step = res[block(e), :] * inverse / center
        s0[block(e), :] = step
        c[block(e), :] = step

    def operate(ref, e):
        cur = ref[block(e), :]
        down_face = fr[block(e), :]
        up_face = above(down_face, fr[block(e - 1), :], first)
        image = sg[block(e), :] * cur
        image += up_face * (cur - above(cur, ref[block(e - 1), :], first))
        image += down_face * (cur - below(cur, ref[block(e + 1), :], last))
        flow = fc[block(e), :] * (cur - pltpu.roll(cur, COLS - 1, 1))
        return cur, image + (flow - pltpu.roll(flow, 1, 1))

    old = 1.0 / ratio
    now, then = s0, s1
    for _sweep in range(SWEEPS - 1):
        new = 1.0 / (2.0 * ratio - old)

        @pl.loop(1, blocks - 1)
        def _(e):
            cur, image = operate(now, e)
            left = res[block(e), :] - image
            res[block(e), :] = left
            step = new * old * cur + (2.0 * new / half_span) * (left * dinv[block(e), :])
            then[block(e), :] = step
            c[block(e), :] += step

        now, then = then, now
        old = new

    def body(i, carry):
        tc, ca = carry
        cur, image = operate(c, i + 2)
        c_out[block(i), :] = cur
        return tc + target[block(i), :] * cur, ca + cur * image

    tc, ca = lax.fori_loop(0, ROWS // 8, body, (zeros, zeros))
    sums[...] = jnp.zeros_like(sums)
    sums[0:1, :] = jnp.full((1, 128), jnp.sum(tc), jnp.float32)
    sums[1:2, :] = jnp.full((1, 128), jnp.sum(ca), jnp.float32)


def chebyshev(target, top, bot, sg, fr, fc):
    return pl.pallas_call(
        chebyshev_kernel,
        in_specs=[VMEM] * 6,
        out_specs=[VMEM] * 2,
        out_shape=[struct(ROWS, COLS), struct(8, 128)],
        scratch_shapes=[pltpu.VMEM((PADDED, COLS), jnp.float32)] * 5,
        compiler_params=LIMIT,
        cost_estimate=pl.CostEstimate(flops=20_000_000, bytes_accessed=4_000_000, transcendentals=0),
    )(target, top, bot, sg, fr, fc)


def step_length(sums):
    return jnp.sum(sums[0:1, 0:1]) / jnp.sum(sums[1:2, 0:1])


def signed():
    tm = lax.axis_index("tm")
    return jnp.where(tm < lax.axis_size("tm") // 2, 1.0, -1.0).astype(jnp.float32)


def correct_kernel(sums, c, out):
    out[...] = step_length(sums) * c[...]


def correct(sums, c):
    return pl.pallas_call(
        correct_kernel,
        in_specs=[VMEM] * 2,
        out_specs=VMEM,
        out_shape=struct(ROWS, COLS),
    )(sums, c)


def first_kernel(p, opposite, correction, out):
    out[...] = p[...] - 0.5 * (p[...] + opposite[...]) + signed() * correction[...][None]


def next_kernel(_, p, opposite, correction, out):
    first_kernel(p, opposite, correction, out)


def update(done, p, opposite, correction, start):
    tile = (STEPS, TILE, COLS)
    at = start // TILE
    specs = [
        pl.BlockSpec(tile, lambda i: (0, at + i, 0)),
        pl.BlockSpec(tile, lambda i: (0, i, 0)),
        pl.BlockSpec((TILE, COLS), lambda i: (at + i, 0)),
    ]
    operands = (p, opposite, correction)
    return pl.pallas_call(
        first_kernel if done is None else next_kernel,
        grid=(opposite.shape[1] // TILE,),
        in_specs=specs if done is None else [ANY] + specs,
        out_specs=pl.BlockSpec(tile, lambda i: (0, at + i, 0)),
        out_shape=struct(STEPS, ROWS, COLS),
        input_output_aliases={} if done is None else {0: 0},
        compiler_params=LIMIT,
    )(*(operands if done is None else (done,) + operands))


def per_device(p, source, offsets, ids, nu_t, sg_t):
    moments = lax.axis_size("tm")
    strips = lax.axis_size("space")
    across = [(i, (i + moments // 2) % moments) for i in range(moments)]
    to_next = [(i, i + 1) for i in range(strips - 1)]
    to_prev = [(j, i) for i, j in to_next]

    early = lax.ppermute(p[:, :EARLY], "tm", across)
    down, up = edges(p, ids)
    top = lax.ppermute(up, "space", to_next)
    bot = lax.ppermute(down, "space", to_prev)
    mine, send, sg, fr, fc = residual(offsets, nu_t, sg_t, p, source, ids, top, bot)

    mine, send = halves(mine, swap(send, 1))
    blocks = merge(mine, swap(send, 2), early, moments // 4)
    x = among_z(total_for_all(among_z(blocks)))
    late = lax.ppermute(gate(p[:, EARLY:], x), "tm", across)
    other = swap(x, 2)
    core_part = swap(jnp.concatenate([x, other]), 1)
    target, first_rows, last_rows = assemble(x, other, core_part)
    t_top = lax.ppermute(last_rows, "space", to_next)
    t_bot = lax.ppermute(first_rows, "space", to_prev)

    c, sums = chebyshev(target, t_top, t_bot, sg, fr, fc)
    every = jnp.broadcast_to(sums[None], (strips,) + sums.shape)
    sums = lax.all_to_all(every, "space", 0, 0).sum(0)
    correction = correct(sums, c)
    updated = update(None, p, early, correction, 0)
    return update(updated, p, late, correction, EARLY), correction


def solution(mesh):
    placed = (P("tm", "space", None), P("tm", "space", None), P("tm"), P("space", None), P(), P())
    return jax.shard_map(
        per_device,
        mesh=mesh,
        in_specs=placed,
        out_specs=(P("tm", "space", None), P("space", None)),
        check_vma=False,
    )
```

```python
import functools

import jax
import jax.numpy as jnp
from jax import lax
from jax.experimental import pallas as pl
from jax.experimental.pallas import tpu as pltpu
from jax.sharding import PartitionSpec as P

SLOT_W = 8
REGIONS = 8
SWEEPS = 4
MINIMUM = 0.2
MAXIMUM = 2.0
ROWS = 128
COLS = 1024
STEPS = 4
EXTENDED = ROWS + 16
CHUNKS = (40, 16, 16, 40, 16)
TILE = 8

ANY = pl.BlockSpec(memory_space=pl.ANY)
VMEM = pl.BlockSpec(memory_space=pltpu.VMEM)
SMEM = pl.BlockSpec(memory_space=pltpu.SMEM)
LIMIT = pltpu.CompilerParams(vmem_limit_bytes=16 * 1024 * 1024)


def struct(*shape):
    return jax.ShapeDtypeStruct(shape, jnp.float32)


def block(i):
    return pl.ds(pl.multiple_of(i * 8, 8), 8)


def harmonic(left, right):
    return 2.0 * left * right / (left + right)


def above(cur, prev, first):
    return jnp.where(first, pltpu.roll(prev, 1, 0), pltpu.roll(cur, 1, 0))


def below(cur, after, last):
    return jnp.where(last, pltpu.roll(after, 7, 0), pltpu.roll(cur, 7, 0))


def row_masks():
    rows = lax.broadcasted_iota(jnp.int32, (8, COLS), 0)
    return rows == 0, rows == 7


def edges_kernel(first_p, last_p, first_ids, last_ids, down_ref, up_ref):
    for out, p, ids, row in ((down_ref, first_p, first_ids, 0), (up_ref, last_p, last_ids, 7)):
        for k in range(STEPS):
            out[k : k + 1, :] = p[k, row : row + 1, :]
            out[STEPS + k : STEPS + k + 1, :] = p[k, row : row + 1, :]
        out[8:16, :] = ids[...].astype(jnp.float32)


def edges(p, ids):
    tail = ROWS // 8 - 1
    return pl.pallas_call(
        edges_kernel,
        grid=(1,),
        in_specs=[
            pl.BlockSpec((STEPS, 8, COLS), lambda i: (0, 0, 0)),
            pl.BlockSpec((STEPS, 8, COLS), lambda i: (0, tail, 0)),
            pl.BlockSpec((8, COLS), lambda i: (0, 0)),
            pl.BlockSpec((8, COLS), lambda i: (tail, 0)),
        ],
        out_specs=[pl.BlockSpec((16, COLS), lambda i: (0, 0))] * 2,
        out_shape=[struct(16, COLS)] * 2,
        compiler_params=LIMIT,
    )(p, p, ids, ids)


def lookup(region, table):
    value = jnp.full(region.shape, table[0], jnp.float32)
    for r in range(1, REGIONS):
        value = jnp.where(region == r, table[r], value)
    return value


def stencil(load, count, fr, sg, fc, use):
    first, last = row_masks()
    cur = load(0)
    cur_up = pltpu.roll(cur, 7, 0)
    flow_before = jnp.zeros((8, COLS), jnp.float32)
    for b in range(count):
        if b + 1 < count:
            after = load(b + 1)
            after_up = pltpu.roll(after, 7, 0)
        else:
            after, after_up = cur, cur_up
        down = fr(b) * (cur - jnp.where(last, after_up, cur_up))
        down_rolled = pltpu.roll(down, 1, 0)
        side = fc(b) * (cur - pltpu.roll(cur, COLS - 1, 1))
        image = sg(b) * cur + (down - jnp.where(first, flow_before, down_rolled))
        image = image + (side - pltpu.roll(side, 1, 1))
        use(b, cur, image)
        cur, cur_up, flow_before = after, after_up, down_rolled


def rows8(b):
    return slice(8 * b, 8 * b + 8)


def residual_kernel(offs, nu_t, sg_t, p, src, ids, acc, nu, sg, fr, fc):
    first, last = row_masks()
    strip, tm = lax.axis_index("space"), lax.axis_index("tm")
    blocks = ROWS // 8
    for b in range(blocks):
        region = ids[rows8(b), :]
        nu[rows8(b), :] = lookup(region, nu_t)
        sg[rows8(b), :] = lookup(region, sg_t)
    for b in range(blocks):
        cur = nu[rows8(b), :]
        after = nu[rows8(min(b + 1, blocks - 1)), :]
        face = harmonic(cur, below(cur, after, last))
        if b == blocks - 1:
            face = jnp.where(last, 0.0, face)
        fr[rows8(b), :] = face
        fc[rows8(b), :] = harmonic(cur, pltpu.roll(cur, COLS - 1, 1))
    scale = signed() / (STEPS * lax.axis_size("tm"))
    acc[...] = jnp.zeros_like(acc)

    @pl.loop(0, STEPS)
    def _(k):
        own = jnp.where(strip < lax.axis_size("space") // 2, offs[k] * SLOT_W, 0)
        back = (-own) & (COLS - 1)

        def use(b, _, image):
            part = src[k, rows8(b), :] - pltpu.roll(image, own, 1)
            acc[rows8(b), :] += scale * part

        stencil(
            lambda b: pltpu.roll(p[k, rows8(b), :], back, 1),
            blocks,
            lambda b: fr[rows8(b), :],
            lambda b: sg[rows8(b), :],
            lambda b: fc[rows8(b), :],
            use,
        )


def residual(offs, nu_t, sg_t, p, src, ids):
    return pl.pallas_call(
        residual_kernel,
        in_specs=[SMEM] * 3 + [VMEM] * 3,
        out_specs=VMEM,
        out_shape=struct(ROWS, COLS),
        scratch_shapes=[pltpu.VMEM((ROWS, COLS), jnp.float32)] * 4,
        compiler_params=LIMIT,
        cost_estimate=pl.CostEstimate(flops=10_000_000, bytes_accessed=20_000_000, transcendentals=0),
    )(offs, nu_t, sg_t, p, src, ids)


def sides_kernel(offs, nu_t, acc, own_first, own_last, top, bot, mine, send):
    strip, tm = lax.axis_index("space"), lax.axis_index("tm")
    half_strips = lax.axis_size("space") // 2
    scale = signed() / (STEPS * lax.axis_size("tm"))
    core, y = tm & 1, (tm >> 1) & 1
    flip = core * 8 + y * 4
    rows = lax.broadcasted_iota(jnp.int32, (8, COLS), 0)
    parts = []
    for own, halo, kind, own_row, halo_row in (
        (own_first, top, strip - 1, 0, 7),
        (own_last, bot, strip + 1, 7, 0),
    ):
        inner = lookup(own[8:16, :], nu_t)[own_row : own_row + 1, :]
        outer = lookup(halo[8:16, :], nu_t)[halo_row : halo_row + 1, :]
        inner = jnp.broadcast_to(inner, (8, COLS))
        outer = jnp.broadcast_to(outer, (8, COLS))
        total = jnp.zeros((8, COLS), jnp.float32)
        for k in range(STEPS):
            turn = offs[k] * SLOT_W
            a = pltpu.roll(inner, jnp.where(strip < half_strips, turn, 0), 1)
            b = pltpu.roll(outer, jnp.where(kind < half_strips, turn, 0), 1)
            gap = own[k : k + 1, :] - halo[k : k + 1, :]
            total = total + harmonic(a, b) * jnp.broadcast_to(gap, (8, COLS))
        parts.append(jnp.where(rows == own_row, scale * total, 0.0))
    for out, shift in ((mine, 0), (send, 8)):
        for i in range(8):
            b = (i + shift) ^ flip
            edge = jnp.where(b == 0, 1.0, 0.0) * parts[0]
            edge = edge + jnp.where(b == ROWS // 8 - 1, 1.0, 0.0) * parts[1]
            out[rows8(i), :] = acc[block(b), :] - edge


def sides(offs, nu_t, acc, own_first, own_last, top, bot):
    return pl.pallas_call(
        sides_kernel,
        in_specs=[SMEM] * 2 + [VMEM] * 5,
        out_specs=[VMEM] * 2,
        out_shape=[struct(ROWS // 2, COLS)] * 2,
        compiler_params=LIMIT,
    )(offs, nu_t, acc, own_first, own_last, top, bot)


def operator_kernel(nu_t, sg_t, ids, top, bot, _, sg, fr, fc, dinv, nu):
    first, last = row_masks()
    strip = lax.axis_index("space")
    blocks = EXTENDED // 8
    for e in range(blocks):
        if e == 0:
            region = top[8:16, :].astype(jnp.int32)
        elif e == blocks - 1:
            region = bot[8:16, :].astype(jnp.int32)
        else:
            region = ids[rows8(e - 1), :]
        nu[rows8(e), :] = lookup(region, nu_t)
        sg[rows8(e), :] = lookup(region, sg_t)
    up = jnp.zeros((8, COLS), jnp.float32)
    for e in range(blocks):
        cur = nu[rows8(e), :]
        face = harmonic(cur, below(cur, nu[rows8(min(e + 1, blocks - 1)), :], last))
        fr[rows8(e), :] = face
        side = harmonic(cur, pltpu.roll(cur, COLS - 1, 1))
        fc[rows8(e), :] = side
        diagonal = sg[rows8(e), :] + above(face, up, first) + face + pltpu.roll(side, 1, 1) + side
        inverse = 1.0 / diagonal
        if e == 0:
            inverse = jnp.where(strip == 0, 0.0, inverse)
        if e == blocks - 1:
            inverse = jnp.where(strip == lax.axis_size("space") - 1, 0.0, inverse)
        dinv[rows8(e), :] = inverse
        up = face


def operator(nu_t, sg_t, ids, top, bot, after):
    return pl.pallas_call(
        operator_kernel,
        in_specs=[SMEM] * 2 + [VMEM] * 3 + [ANY],
        out_specs=[VMEM] * 4,
        out_shape=[struct(EXTENDED, COLS)] * 4,
        scratch_shapes=[pltpu.VMEM((EXTENDED, COLS), jnp.float32)],
        compiler_params=LIMIT,
    )(nu_t, sg_t, ids, top, bot, after)


def swap(x, bit):
    return lax.ppermute(x, "tm", [(i, i ^ bit) for i in range(lax.axis_size("tm"))])


def add_kernel(a, b, mine, send):
    n = mine.shape[0]
    mine[...] = a[:n, :] + b[:n, :]
    send[...] = a[n:, :] + b[n:, :]


def halves(a, b):
    n = a.shape[0] // 2
    return pl.pallas_call(
        add_kernel,
        in_specs=[VMEM] * 2,
        out_specs=[VMEM] * 2,
        out_shape=[struct(n, COLS)] * 2,
        compiler_params=LIMIT,
    )(a, b)


def merge_kernel(a, b, _, out):
    for z in range(out.shape[0]):
        piece = slice(z * 128, z * 128 + 128)
        out[z] = a[:, piece] + b[:, piece]


def merge(a, b, after, count):
    return pl.pallas_call(
        merge_kernel,
        in_specs=[VMEM, VMEM, ANY],
        out_specs=VMEM,
        out_shape=struct(count, a.shape[0], COLS // count),
        compiler_params=LIMIT,
    )(a, b, after)


def total_kernel(parts, out):
    total = parts[0]
    for i in range(1, parts.shape[0]):
        total = total + parts[i]
    for i in range(parts.shape[0]):
        out[i] = total


def total_for_all(parts):
    return pl.pallas_call(
        total_kernel,
        in_specs=[VMEM],
        out_specs=VMEM,
        out_shape=struct(*parts.shape),
        compiler_params=LIMIT,
    )(parts)


def among_z(blocks):
    groups = [[z * 4 + q for z in range(blocks.shape[0])] for q in range(4)]
    return lax.all_to_all(blocks, "tm", 0, 0, axis_index_groups=groups)


def gate_kernel(*_):
    pass


def gate(value, *after):
    return pl.pallas_call(
        gate_kernel,
        in_specs=[ANY] * (1 + len(after)),
        out_specs=ANY,
        out_shape=struct(*value.shape),
        input_output_aliases={0: 0},
        compiler_params=LIMIT,
    )(value, *after)


def edge_kernel(x, out):
    tm = lax.axis_index("tm")
    start = pl.multiple_of(jnp.where((tm & 3) == 0, 0, x.shape[1] - 8), 8)
    out[...] = x[:, pl.ds(start, 8), :]


def edge_rows(x):
    return pl.pallas_call(
        edge_kernel,
        in_specs=[VMEM],
        out_specs=VMEM,
        out_shape=struct(x.shape[0], 8, 128),
        compiler_params=LIMIT,
    )(x)


def for_core_kernel(x, other, edge_a, edge_b, out):
    quarter = x.shape[1]
    out[:, :quarter, :] = x[...]
    out[:, quarter : 2 * quarter, :] = other[...]
    out[:, 2 * quarter :, :] = edge_a[...] + edge_b[...]


def for_core(x, other, edge_a, edge_b):
    return pl.pallas_call(
        for_core_kernel,
        in_specs=[VMEM] * 4,
        out_specs=VMEM,
        out_shape=struct(x.shape[0], 2 * x.shape[1] + 8, 128),
        compiler_params=LIMIT,
    )(x, other, edge_a, edge_b)


def edge_routes(moments, strips):
    routes = []
    for flip in (0, 2):
        route = []
        for z in range(moments // 4):
            for s in range(strips):
                if s > 0:
                    route.append(((z * 4) * strips + s, (z * 4 + 1 + flip) * strips + s - 1))
                if s + 1 < strips:
                    route.append(((z * 4 + 3) * strips + s, (z * 4 + flip) * strips + s + 1))
        routes.append(route)
    return routes


def chebyshev_kernel(own, partner, sg, fr, fc, dinv, c_out, sums, target, res, s0, s1, c):
    tm = lax.axis_index("tm")
    core, y = tm & 1, (tm >> 1) & 1
    flip = core * 8 + y * 4
    blocks = EXTENDED // 8
    for ref, start in ((own, 0), (partner, 8)):
        for z in range(own.shape[0]):
            piece = slice(z * 128, z * 128 + 128)
            for i in range(8):
                target[block(((start + i) ^ flip) + 1), piece] = ref[z, rows8(i), :]
            halo = ref[z, 64:72, :]
            at = jnp.where(core == start // 8, 0, blocks - 1)
            target[block(at), piece] = halo

    center = (MAXIMUM + MINIMUM) / 2.0
    half_span = (MAXIMUM - MINIMUM) / 2.0
    ratio = center / half_span
    for e in range(blocks):
        step = target[rows8(e), :] * dinv[rows8(e), :] / center
        s0[rows8(e), :] = step
        c[rows8(e), :] = step

    def sweep(field, use):
        stencil(
            lambda e: field[rows8(e), :],
            blocks,
            lambda e: fr[rows8(e), :],
            lambda e: sg[rows8(e), :],
            lambda e: fc[rows8(e), :],
            use,
        )

    old = 1.0 / ratio
    now, then = s0, s1
    for number in range(SWEEPS - 1):
        new = 1.0 / (2.0 * ratio - old)

        def use(e, cur, image):
            left = (target if number == 0 else res)[rows8(e), :] - image
            res[rows8(e), :] = left
            step = new * old * cur + (2.0 * new / half_span) * (left * dinv[rows8(e), :])
            then[rows8(e), :] = step
            c[rows8(e), :] += step

        sweep(now, use)
        now, then = then, now
        old = new

    totals = [jnp.zeros((8, COLS), jnp.float32)] * 2

    def finish(e, cur, image):
        if 0 < e < blocks - 1:
            c_out[rows8(e - 1), :] = cur
            totals[0] = totals[0] + target[rows8(e), :] * cur
            totals[1] = totals[1] + cur * image

    sweep(c, finish)
    sums[...] = jnp.zeros_like(sums)
    for i in range(2):
        sums[:, i : i + 1, :] = jnp.full((sums.shape[0], 1, 128), jnp.sum(totals[i]), jnp.float32)


def chebyshev(own, partner, sg, fr, fc, dinv, strips):
    return pl.pallas_call(
        chebyshev_kernel,
        in_specs=[VMEM] * 6,
        out_specs=[VMEM] * 2,
        out_shape=[struct(ROWS, COLS), struct(strips, 8, 128)],
        scratch_shapes=[pltpu.VMEM((EXTENDED, COLS), jnp.float32)] * 5,
        compiler_params=LIMIT,
        cost_estimate=pl.CostEstimate(flops=10_000_000, bytes_accessed=10_000_000, transcendentals=0),
    )(own, partner, sg, fr, fc, dinv)


def step_length(sums):
    every = sums[0]
    for i in range(1, sums.shape[0]):
        every = every + sums[i]
    return jnp.sum(every[0:1, 0:1]) / jnp.sum(every[1:2, 0:1])


def signed():
    tm = lax.axis_index("tm")
    return jnp.where(tm < lax.axis_size("tm") // 2, 1.0, -1.0).astype(jnp.float32)


def correct_kernel(sums, c, out):
    out[...] = step_length(sums) * c[...]


def correct(sums, c):
    return pl.pallas_call(
        correct_kernel,
        in_specs=[VMEM] * 2,
        out_specs=VMEM,
        out_shape=struct(ROWS, COLS),
        compiler_params=LIMIT,
    )(sums, c)


def first_kernel(p, opposite, correction, out):
    out[...] = p[...] - 0.5 * (p[...] + opposite[...]) + signed() * correction[...][None]


def next_kernel(_, p, opposite, correction, out):
    first_kernel(p, opposite, correction, out)


def update(done, p, opposite, correction, start):
    tile = (STEPS, TILE, COLS)
    at = start // TILE
    specs = [
        pl.BlockSpec(tile, lambda i: (0, at + i, 0)),
        pl.BlockSpec(tile, lambda i: (0, i, 0)),
        pl.BlockSpec((TILE, COLS), lambda i: (at + i, 0)),
    ]
    operands = (p, opposite, correction)
    return pl.pallas_call(
        first_kernel if done is None else next_kernel,
        grid=(opposite.shape[1] // TILE,),
        in_specs=specs if done is None else [ANY] + specs,
        out_specs=pl.BlockSpec(tile, lambda i: (0, at + i, 0)),
        out_shape=struct(STEPS, ROWS, COLS),
        input_output_aliases={} if done is None else {0: 0},
        compiler_params=LIMIT,
    )(*(operands if done is None else (done,) + operands))


def per_device(p, source, offsets, ids, nu_t, sg_t):
    moments = lax.axis_size("tm")
    strips = lax.axis_size("space")
    across = [(i, (i + moments // 2) % moments) for i in range(moments)]
    to_next = [(i, i + 1) for i in range(strips - 1)]
    to_prev = [(j, i) for i, j in to_next]
    starts = [sum(CHUNKS[:i]) for i in range(len(CHUNKS))]

    def exchange(i, *after):
        rows = lax.slice_in_dim(p, starts[i], starts[i] + CHUNKS[i], axis=1)
        return lax.ppermute(gate(rows, *after) if after else rows, "tm", across)

    opposite = [exchange(0)]
    down, up = edges(p, ids)
    top = lax.ppermute(up, "space", to_next)
    bot = lax.ppermute(down, "space", to_prev)
    acc = residual(offsets, nu_t, sg_t, p, source, ids)
    mine, send = sides(offsets, nu_t, acc, down, up, top, bot)

    mine, send = halves(mine, swap(send, 1))
    pieces = merge(mine, swap(send, 2), opposite[0], moments // 4)
    opposite.append(exchange(1, pieces))
    total = total_for_all(among_z(pieces))
    opposite.append(exchange(2, total))
    x = among_z(total)
    for i in range(3, len(CHUNKS)):
        opposite.append(exchange(i, x, *opposite[1:3]))
    sg, fr, fc, dinv = operator(nu_t, sg_t, ids, top, bot, x)

    edge = edge_rows(x)
    edge_a, edge_b = (lax.ppermute(edge, ("tm", "space"), r) for r in edge_routes(moments, strips))
    own = for_core(x, swap(x, 2), edge_a, edge_b)
    c, sums = chebyshev(own, swap(own, 1), sg, fr, fc, dinv, strips)
    sums = lax.all_to_all(sums, "space", 0, 0)
    correction = correct(sums, c)
    updated = None
    for start, part in zip(starts, opposite):
        updated = update(updated, p, part, correction, start)
    return updated, correction


def solution(mesh):
    placed = (P("tm", "space", None), P("tm", "space", None), P("tm"), P("space", None), P(), P())
    return jax.shard_map(
        per_device,
        mesh=mesh,
        in_specs=placed,
        out_specs=(P("tm", "space", None), P("space", None)),
        check_vma=False,
    )
```

```python
import functools

import jax
import jax.numpy as jnp
from jax import lax
from jax.experimental import pallas as pl
from jax.experimental.pallas import tpu as pltpu
from jax.sharding import PartitionSpec as P

SLOT_W = 8
REGIONS = 8
SWEEPS = 4
MINIMUM = 0.2
MAXIMUM = 2.0
ROWS = 128
COLS = 1024
STEPS = 4
EXTENDED = ROWS + 16
CHUNKS = (40, 16, 56, 16)

ANY = pl.BlockSpec(memory_space=pl.ANY)
VMEM = pl.BlockSpec(memory_space=pltpu.VMEM)
SMEM = pl.BlockSpec(memory_space=pltpu.SMEM)
LIMIT = pltpu.CompilerParams(vmem_limit_bytes=16 * 1024 * 1024)


def struct(*shape):
    return jax.ShapeDtypeStruct(shape, jnp.float32)


def block(i):
    return pl.ds(pl.multiple_of(i * 8, 8), 8)


def harmonic(left, right):
    return 2.0 * left * right / (left + right)


def above(cur, prev, first):
    return jnp.where(first, pltpu.roll(prev, 1, 0), pltpu.roll(cur, 1, 0))


def below(cur, after, last):
    return jnp.where(last, pltpu.roll(after, 7, 0), pltpu.roll(cur, 7, 0))


def row_masks():
    rows = lax.broadcasted_iota(jnp.int32, (8, COLS), 0)
    return rows == 0, rows == 7


def edges_kernel(first_p, last_p, first_ids, last_ids, down_ref, up_ref):
    for out, p, ids, row in ((down_ref, first_p, first_ids, 0), (up_ref, last_p, last_ids, 7)):
        for k in range(STEPS):
            out[k : k + 1, :] = p[k, row : row + 1, :]
            out[STEPS + k : STEPS + k + 1, :] = p[k, row : row + 1, :]
        out[8:16, :] = ids[...].astype(jnp.float32)


def edges(p, ids):
    tail = ROWS // 8 - 1
    return pl.pallas_call(
        edges_kernel,
        grid=(1,),
        in_specs=[
            pl.BlockSpec((STEPS, 8, COLS), lambda i: (0, 0, 0)),
            pl.BlockSpec((STEPS, 8, COLS), lambda i: (0, tail, 0)),
            pl.BlockSpec((8, COLS), lambda i: (0, 0)),
            pl.BlockSpec((8, COLS), lambda i: (tail, 0)),
        ],
        out_specs=[pl.BlockSpec((16, COLS), lambda i: (0, 0))] * 2,
        out_shape=[struct(16, COLS)] * 2,
        compiler_params=LIMIT,
    )(p, p, ids, ids)


def lookup(region, table):
    value = jnp.full(region.shape, table[0], jnp.float32)
    for r in range(1, REGIONS):
        value = jnp.where(region == r, table[r], value)
    return value


def stencil(load, count, fr, sg, fc, use):
    first, last = row_masks()
    cur = load(0)
    cur_up = pltpu.roll(cur, 7, 0)
    flow_before = jnp.zeros((8, COLS), jnp.float32)
    for b in range(count):
        if b + 1 < count:
            after = load(b + 1)
            after_up = pltpu.roll(after, 7, 0)
        else:
            after, after_up = cur, cur_up
        down = fr(b) * (cur - jnp.where(last, after_up, cur_up))
        down_rolled = pltpu.roll(down, 1, 0)
        side = fc(b) * (cur - pltpu.roll(cur, COLS - 1, 1))
        image = sg(b) * cur + (down - jnp.where(first, flow_before, down_rolled))
        image = image + (side - pltpu.roll(side, 1, 1))
        use(b, cur, image)
        cur, cur_up, flow_before = after, after_up, down_rolled


def rows8(b):
    return slice(8 * b, 8 * b + 8)


def residual_kernel(offs, nu_t, sg_t, p, src, ids, acc, nu, sg, fr, fc):
    first, last = row_masks()
    strip, tm = lax.axis_index("space"), lax.axis_index("tm")
    blocks = ROWS // 8
    for b in range(blocks):
        region = ids[rows8(b), :]
        nu[rows8(b), :] = lookup(region, nu_t)
        sg[rows8(b), :] = lookup(region, sg_t)
    for b in range(blocks):
        cur = nu[rows8(b), :]
        after = nu[rows8(min(b + 1, blocks - 1)), :]
        face = harmonic(cur, below(cur, after, last))
        if b == blocks - 1:
            face = jnp.where(last, 0.0, face)
        fr[rows8(b), :] = face
        fc[rows8(b), :] = harmonic(cur, pltpu.roll(cur, COLS - 1, 1))
    scale = signed() / (STEPS * lax.axis_size("tm"))
    acc[...] = jnp.zeros_like(acc)

    @pl.loop(0, STEPS)
    def _(k):
        own = jnp.where(strip < lax.axis_size("space") // 2, offs[k] * SLOT_W, 0)
        back = (-own) & (COLS - 1)

        def use(b, _, image):
            part = src[k, rows8(b), :] - pltpu.roll(image, own, 1)
            acc[rows8(b), :] += scale * part

        stencil(
            lambda b: pltpu.roll(p[k, rows8(b), :], back, 1),
            blocks,
            lambda b: fr[rows8(b), :],
            lambda b: sg[rows8(b), :],
            lambda b: fc[rows8(b), :],
            use,
        )


def residual(offs, nu_t, sg_t, p, src, ids):
    return pl.pallas_call(
        residual_kernel,
        in_specs=[SMEM] * 3 + [VMEM] * 3,
        out_specs=VMEM,
        out_shape=struct(ROWS, COLS),
        scratch_shapes=[pltpu.VMEM((ROWS, COLS), jnp.float32)] * 4,
        compiler_params=LIMIT,
        cost_estimate=pl.CostEstimate(flops=10_000_000, bytes_accessed=20_000_000, transcendentals=0),
    )(offs, nu_t, sg_t, p, src, ids)


def sides_kernel(offs, nu_t, acc, own_first, own_last, top, bot, mine, send):
    strip, tm = lax.axis_index("space"), lax.axis_index("tm")
    half_strips = lax.axis_size("space") // 2
    scale = signed() / (STEPS * lax.axis_size("tm"))
    core, y = tm & 1, (tm >> 1) & 1
    flip = core * 8 + y * 4
    rows = lax.broadcasted_iota(jnp.int32, (8, COLS), 0)
    parts = []
    for own, halo, kind, own_row, halo_row in (
        (own_first, top, strip - 1, 0, 7),
        (own_last, bot, strip + 1, 7, 0),
    ):
        inner = lookup(own[8:16, :], nu_t)[own_row : own_row + 1, :]
        outer = lookup(halo[8:16, :], nu_t)[halo_row : halo_row + 1, :]
        inner = jnp.broadcast_to(inner, (8, COLS))
        outer = jnp.broadcast_to(outer, (8, COLS))
        total = jnp.zeros((8, COLS), jnp.float32)
        for k in range(STEPS):
            turn = offs[k] * SLOT_W
            a = pltpu.roll(inner, jnp.where(strip < half_strips, turn, 0), 1)
            b = pltpu.roll(outer, jnp.where(kind < half_strips, turn, 0), 1)
            gap = own[k : k + 1, :] - halo[k : k + 1, :]
            total = total + harmonic(a, b) * jnp.broadcast_to(gap, (8, COLS))
        parts.append(jnp.where(rows == own_row, scale * total, 0.0))
    for out, shift in ((mine, 0), (send, 8)):
        for i in range(8):
            b = (i + shift) ^ flip
            edge = jnp.where(b == 0, 1.0, 0.0) * parts[0]
            edge = edge + jnp.where(b == ROWS // 8 - 1, 1.0, 0.0) * parts[1]
            out[rows8(i), :] = acc[block(b), :] - edge


def sides(offs, nu_t, acc, own_first, own_last, top, bot):
    return pl.pallas_call(
        sides_kernel,
        in_specs=[SMEM] * 2 + [VMEM] * 5,
        out_specs=[VMEM] * 2,
        out_shape=[struct(ROWS // 2, COLS)] * 2,
        compiler_params=LIMIT,
    )(offs, nu_t, acc, own_first, own_last, top, bot)


def operator_kernel(nu_t, sg_t, ids, top, bot, _, sg, fr, fc, dinv, nu):
    first, last = row_masks()
    strip = lax.axis_index("space")
    blocks = EXTENDED // 8
    for e in range(blocks):
        if e == 0:
            region = top[8:16, :].astype(jnp.int32)
        elif e == blocks - 1:
            region = bot[8:16, :].astype(jnp.int32)
        else:
            region = ids[rows8(e - 1), :]
        nu[rows8(e), :] = lookup(region, nu_t)
        sg[rows8(e), :] = lookup(region, sg_t)
    up = jnp.zeros((8, COLS), jnp.float32)
    for e in range(blocks):
        cur = nu[rows8(e), :]
        face = harmonic(cur, below(cur, nu[rows8(min(e + 1, blocks - 1)), :], last))
        fr[rows8(e), :] = face
        side = harmonic(cur, pltpu.roll(cur, COLS - 1, 1))
        fc[rows8(e), :] = side
        diagonal = sg[rows8(e), :] + above(face, up, first) + face + pltpu.roll(side, 1, 1) + side
        inverse = 1.0 / diagonal
        if e == 0:
            inverse = jnp.where(strip == 0, 0.0, inverse)
        if e == blocks - 1:
            inverse = jnp.where(strip == lax.axis_size("space") - 1, 0.0, inverse)
        dinv[rows8(e), :] = inverse
        up = face


def operator(nu_t, sg_t, ids, top, bot, after):
    return pl.pallas_call(
        operator_kernel,
        in_specs=[SMEM] * 2 + [VMEM] * 3 + [ANY],
        out_specs=[VMEM] * 4,
        out_shape=[struct(EXTENDED, COLS)] * 4,
        scratch_shapes=[pltpu.VMEM((EXTENDED, COLS), jnp.float32)],
        compiler_params=LIMIT,
    )(nu_t, sg_t, ids, top, bot, after)


def swap(x, bit):
    return lax.ppermute(x, "tm", [(i, i ^ bit) for i in range(lax.axis_size("tm"))])


def add_kernel(a, b, mine, send):
    n = mine.shape[0]
    mine[...] = a[:n, :] + b[:n, :]
    send[...] = a[n:, :] + b[n:, :]


def halves(a, b):
    n = a.shape[0] // 2
    return pl.pallas_call(
        add_kernel,
        in_specs=[VMEM] * 2,
        out_specs=[VMEM] * 2,
        out_shape=[struct(n, COLS)] * 2,
        compiler_params=LIMIT,
    )(a, b)


def merge_kernel(a, b, _, out):
    for z in range(out.shape[0]):
        piece = slice(z * 128, z * 128 + 128)
        out[z] = a[:, piece] + b[:, piece]


def merge(a, b, after, count):
    return pl.pallas_call(
        merge_kernel,
        in_specs=[VMEM, VMEM, ANY],
        out_specs=VMEM,
        out_shape=struct(count, a.shape[0], COLS // count),
        compiler_params=LIMIT,
    )(a, b, after)


def total_kernel(parts, out):
    total = parts[0]
    for i in range(1, parts.shape[0]):
        total = total + parts[i]
    for i in range(parts.shape[0]):
        out[i] = total


def total_for_all(parts):
    return pl.pallas_call(
        total_kernel,
        in_specs=[VMEM],
        out_specs=VMEM,
        out_shape=struct(*parts.shape),
        compiler_params=LIMIT,
    )(parts)


def among_z(blocks):
    groups = [[z * 4 + q for z in range(blocks.shape[0])] for q in range(4)]
    return lax.all_to_all(blocks, "tm", 0, 0, axis_index_groups=groups)


def fetch_kernel(start, p, *refs):
    out = refs[-1]
    out[...] = p[:, start : start + out.shape[1], :]


def fetch(p, start, rows, *after):
    return pl.pallas_call(
        functools.partial(fetch_kernel, start),
        in_specs=[VMEM] + [ANY] * len(after),
        out_specs=VMEM,
        out_shape=struct(STEPS, rows, COLS),
        compiler_params=LIMIT,
    )(p, *after)


def gate_kernel(*_):
    pass


def gate(value, *after):
    return pl.pallas_call(
        gate_kernel,
        in_specs=[ANY] * (1 + len(after)),
        out_specs=ANY,
        out_shape=struct(*value.shape),
        input_output_aliases={0: 0},
        compiler_params=LIMIT,
    )(value, *after)


def edge_kernel(x, out):
    tm = lax.axis_index("tm")
    start = pl.multiple_of(jnp.where((tm & 3) == 0, 0, x.shape[1] - 8), 8)
    out[...] = x[:, pl.ds(start, 8), :]


def edge_rows(x):
    return pl.pallas_call(
        edge_kernel,
        in_specs=[VMEM],
        out_specs=VMEM,
        out_shape=struct(x.shape[0], 8, 128),
        compiler_params=LIMIT,
    )(x)


def for_core_kernel(x, other, edge_a, edge_b, out):
    quarter = x.shape[1]
    out[:, :quarter, :] = x[...]
    out[:, quarter : 2 * quarter, :] = other[...]
    out[:, 2 * quarter :, :] = edge_a[...] + edge_b[...]


def for_core(x, other, edge_a, edge_b):
    return pl.pallas_call(
        for_core_kernel,
        in_specs=[VMEM] * 4,
        out_specs=VMEM,
        out_shape=struct(x.shape[0], 2 * x.shape[1] + 8, 128),
        compiler_params=LIMIT,
    )(x, other, edge_a, edge_b)


def edge_routes(moments, strips):
    routes = []
    for flip in (0, 2):
        route = []
        for z in range(moments // 4):
            for s in range(strips):
                if s > 0:
                    route.append(((z * 4) * strips + s, (z * 4 + 1 + flip) * strips + s - 1))
                if s + 1 < strips:
                    route.append(((z * 4 + 3) * strips + s, (z * 4 + flip) * strips + s + 1))
        routes.append(route)
    return routes


def chebyshev_kernel(own, partner, sg, fr, fc, dinv, c_out, sums, target, res, s0, s1, c):
    tm = lax.axis_index("tm")
    core, y = tm & 1, (tm >> 1) & 1
    flip = core * 8 + y * 4
    blocks = EXTENDED // 8
    for ref, start in ((own, 0), (partner, 8)):
        for z in range(own.shape[0]):
            piece = slice(z * 128, z * 128 + 128)
            for i in range(8):
                target[block(((start + i) ^ flip) + 1), piece] = ref[z, rows8(i), :]
            halo = ref[z, 64:72, :]
            at = jnp.where(core == start // 8, 0, blocks - 1)
            target[block(at), piece] = halo

    center = (MAXIMUM + MINIMUM) / 2.0
    half_span = (MAXIMUM - MINIMUM) / 2.0
    ratio = center / half_span
    for e in range(blocks):
        step = target[rows8(e), :] * dinv[rows8(e), :] / center
        s0[rows8(e), :] = step
        c[rows8(e), :] = step

    def sweep(field, use):
        stencil(
            lambda e: field[rows8(e), :],
            blocks,
            lambda e: fr[rows8(e), :],
            lambda e: sg[rows8(e), :],
            lambda e: fc[rows8(e), :],
            use,
        )

    old = 1.0 / ratio
    now, then = s0, s1
    for number in range(SWEEPS - 1):
        new = 1.0 / (2.0 * ratio - old)

        def use(e, cur, image):
            left = (target if number == 0 else res)[rows8(e), :] - image
            res[rows8(e), :] = left
            step = new * old * cur + (2.0 * new / half_span) * (left * dinv[rows8(e), :])
            then[rows8(e), :] = step
            c[rows8(e), :] += step

        sweep(now, use)
        now, then = then, now
        old = new

    totals = [jnp.zeros((8, COLS), jnp.float32)] * 2

    def finish(e, cur, image):
        if 0 < e < blocks - 1:
            c_out[rows8(e - 1), :] = cur
            totals[0] = totals[0] + target[rows8(e), :] * cur
            totals[1] = totals[1] + cur * image

    sweep(c, finish)
    sums[...] = jnp.zeros_like(sums)
    for i in range(2):
        sums[:, i : i + 1, :] = jnp.full((sums.shape[0], 1, 128), jnp.sum(totals[i]), jnp.float32)


def chebyshev(own, partner, sg, fr, fc, dinv, strips):
    return pl.pallas_call(
        chebyshev_kernel,
        in_specs=[VMEM] * 6,
        out_specs=[VMEM] * 2,
        out_shape=[struct(ROWS, COLS), struct(strips, 8, 128)],
        scratch_shapes=[pltpu.VMEM((EXTENDED, COLS), jnp.float32)] * 5,
        compiler_params=LIMIT,
        cost_estimate=pl.CostEstimate(flops=10_000_000, bytes_accessed=10_000_000, transcendentals=0),
    )(own, partner, sg, fr, fc, dinv)


def step_length(sums):
    every = sums[0]
    for i in range(1, sums.shape[0]):
        every = every + sums[i]
    return jnp.sum(every[0:1, 0:1]) / jnp.sum(every[1:2, 0:1])


def signed():
    tm = lax.axis_index("tm")
    return jnp.where(tm < lax.axis_size("tm") // 2, 1.0, -1.0).astype(jnp.float32)


def update_kernel(starts, fresh, *refs):
    refs = refs if fresh else refs[1:]
    sums, c, p = refs[:3]
    opposite, refs = refs[3 : 3 + len(starts)], refs[3 + len(starts) :]
    if fresh:
        out, correction, buffer, kept, out_sem, kept_sem = refs
    else:
        out, buffer, out_sem = refs
    omega, sign = step_length(sums), signed()
    copies = []
    for i, (start, part) in enumerate(zip(starts, opposite)):
        for r in range(0, part.shape[1], 8):
            here = slice(start + r, start + r + 8)
            corrected = omega * c[here, :]
            for k in range(STEPS):
                field = p[k, here, :]
                moved = field - 0.5 * (field + part[k, r : r + 8, :])
                buffer[k, here, :] = moved + sign * corrected
        rows = pl.ds(start, part.shape[1])
        copies.append(pltpu.make_async_copy(buffer.at[:, rows], out.at[:, rows], out_sem.at[i]))
        copies[-1].start()
    if fresh:
        kept[...] = omega * c[...]
        copies.append(pltpu.make_async_copy(kept, correction, kept_sem))
        copies[-1].start()
    for copy in copies:
        copy.wait()


def update(done, sums, c, p, opposite, starts):
    fresh = done is None
    shape, strip = (STEPS, ROWS, COLS), (ROWS, COLS)
    sems = pltpu.SemaphoreType.DMA((len(starts),))
    buffer = pltpu.VMEM(shape, jnp.float32)
    operands = (sums, c, p, *opposite)
    return pl.pallas_call(
        functools.partial(update_kernel, starts, fresh),
        in_specs=([] if fresh else [ANY]) + [VMEM] * len(operands),
        out_specs=[ANY] * 2 if fresh else ANY,
        out_shape=[struct(*shape), struct(*strip)] if fresh else struct(*shape),
        scratch_shapes=(
            [buffer, pltpu.VMEM(strip, jnp.float32), sems, pltpu.SemaphoreType.DMA]
            if fresh
            else [buffer, sems]
        ),
        input_output_aliases={} if fresh else {0: 0},
        compiler_params=LIMIT,
    )(*(operands if fresh else (done,) + operands))


def per_device(p, source, offsets, ids, nu_t, sg_t):
    moments = lax.axis_size("tm")
    strips = lax.axis_size("space")
    across = [(i, (i + moments // 2) % moments) for i in range(moments)]
    to_next = [(i, i + 1) for i in range(strips - 1)]
    to_prev = [(j, i) for i, j in to_next]
    starts = [sum(CHUNKS[:i]) for i in range(len(CHUNKS))]

    def exchange(i, *after):
        return lax.ppermute(fetch(p, starts[i], CHUNKS[i], *after), "tm", across)

    def ready(i, *after):
        rows = lax.slice_in_dim(p, starts[i], starts[i] + CHUNKS[i], axis=1)
        return lax.ppermute(gate(rows, *after), "tm", across)

    opposite = [lax.ppermute(p[:, : CHUNKS[0]], "tm", across)]
    down, up = edges(p, ids)
    top = lax.ppermute(up, "space", to_next)
    bot = lax.ppermute(down, "space", to_prev)
    acc = residual(offsets, nu_t, sg_t, p, source, ids)
    mine, send = sides(offsets, nu_t, acc, down, up, top, bot)

    mine, send = halves(mine, swap(send, 1))
    pieces = merge(mine, swap(send, 2), opposite[0], moments // 4)
    opposite.append(ready(1, pieces))
    total = total_for_all(among_z(pieces))
    x = among_z(total)
    for i in range(2, len(CHUNKS)):
        opposite.append(ready(i, x, opposite[1]))
    sg, fr, fc, dinv = operator(nu_t, sg_t, ids, top, bot, x)

    edge = edge_rows(x)
    edge_a, edge_b = (lax.ppermute(edge, ("tm", "space"), r) for r in edge_routes(moments, strips))
    own = for_core(x, swap(x, 2), edge_a, edge_b)
    c, sums = chebyshev(own, swap(own, 1), sg, fr, fc, dinv, strips)
    sums = lax.all_to_all(sums, "space", 0, 0)
    updated, correction = update(None, sums, c, p, opposite[:-1], starts[:-1])
    return update(updated, sums, c, p, opposite[-1:], starts[-1:]), correction


def solution(mesh):
    placed = (P("tm", "space", None), P("tm", "space", None), P("tm"), P("space", None), P(), P())
    return jax.shard_map(
        per_device,
        mesh=mesh,
        in_specs=placed,
        out_specs=(P("tm", "space", None), P("space", None)),
        check_vma=False,
    )
```

```python
import functools

import jax
import jax.numpy as jnp
from jax import lax
from jax.experimental import pallas as pl
from jax.experimental.pallas import tpu as pltpu
from jax.sharding import PartitionSpec as P

SLOT_W = 8
REGIONS = 8
SWEEPS = 4
MINIMUM = 0.2
MAXIMUM = 2.0
ROWS = 128
COLS = 1024
STEPS = 4
EXTENDED = ROWS + 16
CHUNKS = (40, 16, 16, 32, 24)

ANY = pl.BlockSpec(memory_space=pl.ANY)
VMEM = pl.BlockSpec(memory_space=pltpu.VMEM)
SMEM = pl.BlockSpec(memory_space=pltpu.SMEM)
LIMIT = pltpu.CompilerParams(vmem_limit_bytes=16 * 1024 * 1024)


def struct(*shape):
    return jax.ShapeDtypeStruct(shape, jnp.float32)


def block(i):
    return pl.ds(pl.multiple_of(i * 8, 8), 8)


def harmonic(left, right):
    return 2.0 * left * right / (left + right)


def above(cur, prev, first):
    return jnp.where(first, pltpu.roll(prev, 1, 0), pltpu.roll(cur, 1, 0))


def below(cur, after, last):
    return jnp.where(last, pltpu.roll(after, 7, 0), pltpu.roll(cur, 7, 0))


def row_masks():
    rows = lax.broadcasted_iota(jnp.int32, (8, COLS), 0)
    return rows == 0, rows == 7


def edges_kernel(first_p, last_p, first_ids, last_ids, down_ref, up_ref):
    for out, p, ids, row in ((down_ref, first_p, first_ids, 0), (up_ref, last_p, last_ids, 7)):
        for k in range(STEPS):
            out[k : k + 1, :] = p[k, row : row + 1, :]
            out[STEPS + k : STEPS + k + 1, :] = p[k, row : row + 1, :]
        out[8:16, :] = ids[...].astype(jnp.float32)


def edges(p, ids):
    tail = ROWS // 8 - 1
    return pl.pallas_call(
        edges_kernel,
        grid=(1,),
        in_specs=[
            pl.BlockSpec((STEPS, 8, COLS), lambda i: (0, 0, 0)),
            pl.BlockSpec((STEPS, 8, COLS), lambda i: (0, tail, 0)),
            pl.BlockSpec((8, COLS), lambda i: (0, 0)),
            pl.BlockSpec((8, COLS), lambda i: (tail, 0)),
        ],
        out_specs=[pl.BlockSpec((16, COLS), lambda i: (0, 0))] * 2,
        out_shape=[struct(16, COLS)] * 2,
        compiler_params=LIMIT,
    )(p, p, ids, ids)


def lookup(region, table):
    value = jnp.full(region.shape, table[0], jnp.float32)
    for r in range(1, REGIONS):
        value = jnp.where(region == r, table[r], value)
    return value


def stencil(load, count, fr, sg, fc, use):
    first, last = row_masks()
    cur = load(0)
    cur_up = pltpu.roll(cur, 7, 0)
    flow_before = jnp.zeros((8, COLS), jnp.float32)
    for b in range(count):
        if b + 1 < count:
            after = load(b + 1)
            after_up = pltpu.roll(after, 7, 0)
        else:
            after, after_up = cur, cur_up
        down = fr(b) * (cur - jnp.where(last, after_up, cur_up))
        down_rolled = pltpu.roll(down, 1, 0)
        side = fc(b) * (cur - pltpu.roll(cur, COLS - 1, 1))
        image = sg(b) * cur + (down - jnp.where(first, flow_before, down_rolled))
        image = image + (side - pltpu.roll(side, 1, 1))
        use(b, cur, image)
        cur, cur_up, flow_before = after, after_up, down_rolled


def rows8(b):
    return slice(8 * b, 8 * b + 8)


def residual_kernel(offs, nu_t, sg_t, p, src, ids, acc, nu, sg, fr, fc):
    first, last = row_masks()
    strip, tm = lax.axis_index("space"), lax.axis_index("tm")
    blocks = ROWS // 8
    for b in range(blocks):
        region = ids[rows8(b), :]
        nu[rows8(b), :] = lookup(region, nu_t)
        sg[rows8(b), :] = lookup(region, sg_t)
    for b in range(blocks):
        cur = nu[rows8(b), :]
        after = nu[rows8(min(b + 1, blocks - 1)), :]
        face = harmonic(cur, below(cur, after, last))
        if b == blocks - 1:
            face = jnp.where(last, 0.0, face)
        fr[rows8(b), :] = face
        fc[rows8(b), :] = harmonic(cur, pltpu.roll(cur, COLS - 1, 1))
    scale = signed() / (STEPS * lax.axis_size("tm"))
    acc[...] = jnp.zeros_like(acc)

    @pl.loop(0, STEPS)
    def _(k):
        own = jnp.where(strip < lax.axis_size("space") // 2, offs[k] * SLOT_W, 0)
        back = (-own) & (COLS - 1)

        def use(b, _, image):
            part = src[k, rows8(b), :] - pltpu.roll(image, own, 1)
            acc[rows8(b), :] += scale * part

        stencil(
            lambda b: pltpu.roll(p[k, rows8(b), :], back, 1),
            blocks,
            lambda b: fr[rows8(b), :],
            lambda b: sg[rows8(b), :],
            lambda b: fc[rows8(b), :],
            use,
        )


def residual(offs, nu_t, sg_t, p, src, ids):
    return pl.pallas_call(
        residual_kernel,
        in_specs=[SMEM] * 3 + [VMEM] * 3,
        out_specs=VMEM,
        out_shape=struct(ROWS, COLS),
        scratch_shapes=[pltpu.VMEM((ROWS, COLS), jnp.float32)] * 4,
        compiler_params=LIMIT,
        cost_estimate=pl.CostEstimate(flops=10_000_000, bytes_accessed=20_000_000, transcendentals=0),
    )(offs, nu_t, sg_t, p, src, ids)


def sides_kernel(offs, nu_t, acc, own_first, own_last, top, bot, mine, send):
    strip, tm = lax.axis_index("space"), lax.axis_index("tm")
    half_strips = lax.axis_size("space") // 2
    scale = signed() / (STEPS * lax.axis_size("tm"))
    core, y = tm & 1, (tm >> 1) & 1
    flip = core * 8 + y * 4
    rows = lax.broadcasted_iota(jnp.int32, (8, COLS), 0)
    parts = []
    for own, halo, kind, own_row, halo_row in (
        (own_first, top, strip - 1, 0, 7),
        (own_last, bot, strip + 1, 7, 0),
    ):
        inner = lookup(own[8:16, :], nu_t)[own_row : own_row + 1, :]
        outer = lookup(halo[8:16, :], nu_t)[halo_row : halo_row + 1, :]
        inner = jnp.broadcast_to(inner, (8, COLS))
        outer = jnp.broadcast_to(outer, (8, COLS))
        total = jnp.zeros((8, COLS), jnp.float32)
        for k in range(STEPS):
            turn = offs[k] * SLOT_W
            a = pltpu.roll(inner, jnp.where(strip < half_strips, turn, 0), 1)
            b = pltpu.roll(outer, jnp.where(kind < half_strips, turn, 0), 1)
            gap = own[k : k + 1, :] - halo[k : k + 1, :]
            total = total + harmonic(a, b) * jnp.broadcast_to(gap, (8, COLS))
        parts.append(jnp.where(rows == own_row, scale * total, 0.0))
    for out, shift in ((mine, 0), (send, 8)):
        for i in range(8):
            b = (i + shift) ^ flip
            edge = jnp.where(b == 0, 1.0, 0.0) * parts[0]
            edge = edge + jnp.where(b == ROWS // 8 - 1, 1.0, 0.0) * parts[1]
            out[rows8(i), :] = acc[block(b), :] - edge


def sides(offs, nu_t, acc, own_first, own_last, top, bot):
    return pl.pallas_call(
        sides_kernel,
        in_specs=[SMEM] * 2 + [VMEM] * 5,
        out_specs=[VMEM] * 2,
        out_shape=[struct(ROWS // 2, COLS)] * 2,
        compiler_params=LIMIT,
    )(offs, nu_t, acc, own_first, own_last, top, bot)


def operator_kernel(nu_t, sg_t, ids, top, bot, _, sg, fr, fc, dinv, nu):
    first, last = row_masks()
    strip = lax.axis_index("space")
    blocks = EXTENDED // 8
    for e in range(blocks):
        if e == 0:
            region = top[8:16, :].astype(jnp.int32)
        elif e == blocks - 1:
            region = bot[8:16, :].astype(jnp.int32)
        else:
            region = ids[rows8(e - 1), :]
        nu[rows8(e), :] = lookup(region, nu_t)
        sg[rows8(e), :] = lookup(region, sg_t)
    up = jnp.zeros((8, COLS), jnp.float32)
    for e in range(blocks):
        cur = nu[rows8(e), :]
        face = harmonic(cur, below(cur, nu[rows8(min(e + 1, blocks - 1)), :], last))
        fr[rows8(e), :] = face
        side = harmonic(cur, pltpu.roll(cur, COLS - 1, 1))
        fc[rows8(e), :] = side
        diagonal = sg[rows8(e), :] + above(face, up, first) + face + pltpu.roll(side, 1, 1) + side
        inverse = 1.0 / diagonal
        if e == 0:
            inverse = jnp.where(strip == 0, 0.0, inverse)
        if e == blocks - 1:
            inverse = jnp.where(strip == lax.axis_size("space") - 1, 0.0, inverse)
        dinv[rows8(e), :] = inverse
        up = face


def operator(nu_t, sg_t, ids, top, bot, after):
    return pl.pallas_call(
        operator_kernel,
        in_specs=[SMEM] * 2 + [VMEM] * 3 + [ANY],
        out_specs=[VMEM] * 4,
        out_shape=[struct(EXTENDED, COLS)] * 4,
        scratch_shapes=[pltpu.VMEM((EXTENDED, COLS), jnp.float32)],
        compiler_params=LIMIT,
    )(nu_t, sg_t, ids, top, bot, after)


def swap(x, bit):
    return lax.ppermute(x, "tm", [(i, i ^ bit) for i in range(lax.axis_size("tm"))])


def add_kernel(a, b, mine, send):
    n = mine.shape[0]
    mine[...] = a[:n, :] + b[:n, :]
    send[...] = a[n:, :] + b[n:, :]


def halves(a, b):
    n = a.shape[0] // 2
    return pl.pallas_call(
        add_kernel,
        in_specs=[VMEM] * 2,
        out_specs=[VMEM] * 2,
        out_shape=[struct(n, COLS)] * 2,
        compiler_params=LIMIT,
    )(a, b)


def merge_kernel(a, b, _, out):
    for z in range(out.shape[0]):
        piece = slice(z * 128, z * 128 + 128)
        out[z] = a[:, piece] + b[:, piece]


def merge(a, b, after, count):
    return pl.pallas_call(
        merge_kernel,
        in_specs=[VMEM, VMEM, ANY],
        out_specs=VMEM,
        out_shape=struct(count, a.shape[0], COLS // count),
        compiler_params=LIMIT,
    )(a, b, after)


def total_kernel(parts, out):
    total = parts[0]
    for i in range(1, parts.shape[0]):
        total = total + parts[i]
    for i in range(parts.shape[0]):
        out[i] = total


def total_for_all(parts):
    return pl.pallas_call(
        total_kernel,
        in_specs=[VMEM],
        out_specs=VMEM,
        out_shape=struct(*parts.shape),
        compiler_params=LIMIT,
    )(parts)


def among_z(blocks):
    groups = [[z * 4 + q for z in range(blocks.shape[0])] for q in range(4)]
    return lax.all_to_all(blocks, "tm", 0, 0, axis_index_groups=groups)


def gate_kernel(*_):
    pass


def gate(value, *after):
    return pl.pallas_call(
        gate_kernel,
        in_specs=[ANY] * (1 + len(after)),
        out_specs=ANY,
        out_shape=struct(*value.shape),
        input_output_aliases={0: 0},
        compiler_params=LIMIT,
    )(value, *after)


def edge_kernel(x, out):
    tm = lax.axis_index("tm")
    start = pl.multiple_of(jnp.where((tm & 3) == 0, 0, x.shape[1] - 8), 8)
    out[...] = x[:, pl.ds(start, 8), :]


def edge_rows(x):
    return pl.pallas_call(
        edge_kernel,
        in_specs=[VMEM],
        out_specs=VMEM,
        out_shape=struct(x.shape[0], 8, 128),
        compiler_params=LIMIT,
    )(x)


def for_core_kernel(x, other, edge_a, edge_b, out):
    quarter = x.shape[1]
    out[:, :quarter, :] = x[...]
    out[:, quarter : 2 * quarter, :] = other[...]
    out[:, 2 * quarter :, :] = edge_a[...] + edge_b[...]


def for_core(x, other, edge_a, edge_b):
    return pl.pallas_call(
        for_core_kernel,
        in_specs=[VMEM] * 4,
        out_specs=VMEM,
        out_shape=struct(x.shape[0], 2 * x.shape[1] + 8, 128),
        compiler_params=LIMIT,
    )(x, other, edge_a, edge_b)


def edge_routes(moments, strips):
    routes = []
    for flip in (0, 2):
        route = []
        for z in range(moments // 4):
            for s in range(strips):
                if s > 0:
                    route.append(((z * 4) * strips + s, (z * 4 + 1 + flip) * strips + s - 1))
                if s + 1 < strips:
                    route.append(((z * 4 + 3) * strips + s, (z * 4 + flip) * strips + s + 1))
        routes.append(route)
    return routes


def chebyshev_kernel(own, partner, sg, fr, fc, dinv, c_out, sums, target, res, s0, s1, c):
    tm = lax.axis_index("tm")
    core, y = tm & 1, (tm >> 1) & 1
    flip = core * 8 + y * 4
    blocks = EXTENDED // 8
    for ref, start in ((own, 0), (partner, 8)):
        for z in range(own.shape[0]):
            piece = slice(z * 128, z * 128 + 128)
            for i in range(8):
                target[block(((start + i) ^ flip) + 1), piece] = ref[z, rows8(i), :]
            halo = ref[z, 64:72, :]
            at = jnp.where(core == start // 8, 0, blocks - 1)
            target[block(at), piece] = halo

    center = (MAXIMUM + MINIMUM) / 2.0
    half_span = (MAXIMUM - MINIMUM) / 2.0
    ratio = center / half_span
    for e in range(blocks):
        step = target[rows8(e), :] * dinv[rows8(e), :] / center
        s0[rows8(e), :] = step
        c[rows8(e), :] = step

    def sweep(field, use):
        stencil(
            lambda e: field[rows8(e), :],
            blocks,
            lambda e: fr[rows8(e), :],
            lambda e: sg[rows8(e), :],
            lambda e: fc[rows8(e), :],
            use,
        )

    old = 1.0 / ratio
    now, then = s0, s1
    for number in range(SWEEPS - 1):
        new = 1.0 / (2.0 * ratio - old)

        def use(e, cur, image):
            left = (target if number == 0 else res)[rows8(e), :] - image
            res[rows8(e), :] = left
            step = new * old * cur + (2.0 * new / half_span) * (left * dinv[rows8(e), :])
            then[rows8(e), :] = step
            c[rows8(e), :] += step

        sweep(now, use)
        now, then = then, now
        old = new

    totals = [jnp.zeros((8, COLS), jnp.float32)] * 2

    def finish(e, cur, image):
        if 0 < e < blocks - 1:
            c_out[rows8(e - 1), :] = cur
            totals[0] = totals[0] + target[rows8(e), :] * cur
            totals[1] = totals[1] + cur * image

    sweep(c, finish)
    sums[...] = jnp.zeros_like(sums)
    for i in range(2):
        sums[:, i : i + 1, :] = jnp.full((sums.shape[0], 1, 128), jnp.sum(totals[i]), jnp.float32)


def chebyshev(own, partner, sg, fr, fc, dinv, strips):
    return pl.pallas_call(
        chebyshev_kernel,
        in_specs=[VMEM] * 6,
        out_specs=[VMEM] * 2,
        out_shape=[struct(ROWS, COLS), struct(strips, 8, 128)],
        scratch_shapes=[pltpu.VMEM((EXTENDED, COLS), jnp.float32)] * 5,
        compiler_params=LIMIT,
        cost_estimate=pl.CostEstimate(flops=10_000_000, bytes_accessed=10_000_000, transcendentals=0),
    )(own, partner, sg, fr, fc, dinv)


def step_length(sums):
    every = sums[0]
    for i in range(1, sums.shape[0]):
        every = every + sums[i]
    return jnp.sum(every[0:1, 0:1]) / jnp.sum(every[1:2, 0:1])


def signed():
    tm = lax.axis_index("tm")
    return jnp.where(tm < lax.axis_size("tm") // 2, 1.0, -1.0).astype(jnp.float32)


def update_kernel(starts, fresh, *refs):
    refs = refs if fresh else refs[1:]
    sums, c, p = refs[:3]
    opposite, refs = refs[3 : 3 + len(starts)], refs[3 + len(starts) :]
    if fresh:
        out, correction, buffer, kept, out_sem, kept_sem = refs
    else:
        out, buffer, out_sem = refs
    omega, sign = step_length(sums), signed()
    copies = []
    for i, (start, part) in enumerate(zip(starts, opposite)):
        for r in range(0, part.shape[1], 8):
            here = slice(start + r, start + r + 8)
            corrected = omega * c[here, :]
            for k in range(STEPS):
                field = p[k, here, :]
                moved = field - 0.5 * (field + part[k, r : r + 8, :])
                buffer[k, here, :] = moved + sign * corrected
        rows = pl.ds(start, part.shape[1])
        copies.append(pltpu.make_async_copy(buffer.at[:, rows], out.at[:, rows], out_sem.at[i]))
        copies[-1].start()
    if fresh:
        kept[...] = omega * c[...]
        copies.append(pltpu.make_async_copy(kept, correction, kept_sem))
        copies[-1].start()
    for copy in copies:
        copy.wait()


def update(done, sums, c, p, opposite, starts):
    fresh = done is None
    shape, strip = (STEPS, ROWS, COLS), (ROWS, COLS)
    sems = pltpu.SemaphoreType.DMA((len(starts),))
    buffer = pltpu.VMEM(shape, jnp.float32)
    operands = (sums, c, p, *opposite)
    return pl.pallas_call(
        functools.partial(update_kernel, starts, fresh),
        in_specs=([] if fresh else [ANY]) + [VMEM] * len(operands),
        out_specs=[ANY] * 2 if fresh else ANY,
        out_shape=[struct(*shape), struct(*strip)] if fresh else struct(*shape),
        scratch_shapes=(
            [buffer, pltpu.VMEM(strip, jnp.float32), sems, pltpu.SemaphoreType.DMA]
            if fresh
            else [buffer, sems]
        ),
        input_output_aliases={} if fresh else {0: 0},
        compiler_params=LIMIT,
    )(*(operands if fresh else (done,) + operands))


def per_device(p, source, offsets, ids, nu_t, sg_t):
    moments = lax.axis_size("tm")
    strips = lax.axis_size("space")
    across = [(i, (i + moments // 2) % moments) for i in range(moments)]
    to_next = [(i, i + 1) for i in range(strips - 1)]
    to_prev = [(j, i) for i, j in to_next]
    starts = [sum(CHUNKS[:i]) for i in range(len(CHUNKS))]

    def ready(i, *after):
        rows = lax.slice_in_dim(p, starts[i], starts[i] + CHUNKS[i], axis=1)
        return lax.ppermute(gate(rows, *after), "tm", across)

    opposite = [lax.ppermute(p[:, : CHUNKS[0]], "tm", across)]
    down, up = edges(p, ids)
    top = lax.ppermute(up, "space", to_next)
    bot = lax.ppermute(down, "space", to_prev)
    acc = residual(offsets, nu_t, sg_t, p, source, ids)
    mine, send = sides(offsets, nu_t, acc, down, up, top, bot)

    mine, send = halves(mine, swap(send, 1))
    pieces = merge(mine, swap(send, 2), opposite[0], moments // 4)
    opposite.append(ready(1, pieces))
    total = total_for_all(among_z(pieces))
    opposite.append(ready(2, opposite[1]))
    x = among_z(total)
    for i in range(3, len(CHUNKS)):
        opposite.append(ready(i, x, opposite[2]))
    sg, fr, fc, dinv = operator(nu_t, sg_t, ids, top, bot, x)

    edge = edge_rows(x)
    edge_a, edge_b = (lax.ppermute(edge, ("tm", "space"), r) for r in edge_routes(moments, strips))
    own = for_core(x, swap(x, 2), edge_a, edge_b)
    c, sums = chebyshev(own, swap(own, 1), sg, fr, fc, dinv, strips)
    sums = lax.all_to_all(sums, "space", 0, 0)
    updated, correction = update(None, sums, c, p, opposite[:-1], starts[:-1])
    return update(updated, sums, c, p, opposite[-1:], starts[-1:]), correction


def solution(mesh):
    placed = (P("tm", "space", None), P("tm", "space", None), P("tm"), P("space", None), P(), P())
    return jax.shard_map(
        per_device,
        mesh=mesh,
        in_specs=placed,
        out_specs=(P("tm", "space", None), P("space", None)),
        check_vma=False,
    )
```

```python
import functools

import jax
import jax.numpy as jnp
from jax import lax
from jax.experimental import pallas as pl
from jax.experimental.pallas import tpu as pltpu
from jax.sharding import PartitionSpec as P

SLOT_W = 8
REGIONS = 8
SWEEPS = 4
MINIMUM = 0.2
MAXIMUM = 2.0
ROWS = 128
COLS = 1024
STEPS = 4
EXTENDED = ROWS + 16
CHUNKS = (40, 16, 16, 32, 24)

ANY = pl.BlockSpec(memory_space=pl.ANY)
VMEM = pl.BlockSpec(memory_space=pltpu.VMEM)
SMEM = pl.BlockSpec(memory_space=pltpu.SMEM)
LIMIT = pltpu.CompilerParams(vmem_limit_bytes=16 * 1024 * 1024)


def struct(*shape):
    return jax.ShapeDtypeStruct(shape, jnp.float32)


def block(i):
    return pl.ds(pl.multiple_of(i * 8, 8), 8)


def harmonic(left, right):
    return 2.0 * left * right / (left + right)


def above(cur, prev, first):
    return jnp.where(first, pltpu.roll(prev, 1, 0), pltpu.roll(cur, 1, 0))


def below(cur, after, last):
    return jnp.where(last, pltpu.roll(after, 7, 0), pltpu.roll(cur, 7, 0))


def row_masks():
    rows = lax.broadcasted_iota(jnp.int32, (8, COLS), 0)
    return rows == 0, rows == 7


def edges_kernel(first_p, last_p, first_ids, last_ids, down_ref, up_ref):
    for out, p, ids, row in ((down_ref, first_p, first_ids, 0), (up_ref, last_p, last_ids, 7)):
        for k in range(STEPS):
            out[k : k + 1, :] = p[k, row : row + 1, :]
            out[STEPS + k : STEPS + k + 1, :] = p[k, row : row + 1, :]
        out[8:16, :] = ids[...].astype(jnp.float32)


def edges(p, ids):
    tail = ROWS // 8 - 1
    return pl.pallas_call(
        edges_kernel,
        grid=(1,),
        in_specs=[
            pl.BlockSpec((STEPS, 8, COLS), lambda i: (0, 0, 0)),
            pl.BlockSpec((STEPS, 8, COLS), lambda i: (0, tail, 0)),
            pl.BlockSpec((8, COLS), lambda i: (0, 0)),
            pl.BlockSpec((8, COLS), lambda i: (tail, 0)),
        ],
        out_specs=[pl.BlockSpec((16, COLS), lambda i: (0, 0))] * 2,
        out_shape=[struct(16, COLS)] * 2,
        compiler_params=LIMIT,
    )(p, p, ids, ids)


def lookup(region, table):
    value = jnp.full(region.shape, table[0], jnp.float32)
    for r in range(1, REGIONS):
        value = jnp.where(region == r, table[r], value)
    return value


def stencil(load, count, fr, sg, fc, use):
    first, last = row_masks()
    cur = load(0)
    cur_up = pltpu.roll(cur, 7, 0)
    flow_before = jnp.zeros((8, COLS), jnp.float32)
    for b in range(count):
        if b + 1 < count:
            after = load(b + 1)
            after_up = pltpu.roll(after, 7, 0)
        else:
            after, after_up = cur, cur_up
        down = fr(b) * (cur - jnp.where(last, after_up, cur_up))
        down_rolled = pltpu.roll(down, 1, 0)
        side = fc(b) * (cur - pltpu.roll(cur, COLS - 1, 1))
        image = sg(b) * cur + (down - jnp.where(first, flow_before, down_rolled))
        image = image + (side - pltpu.roll(side, 1, 1))
        use(b, cur, image)
        cur, cur_up, flow_before = after, after_up, down_rolled


def rows8(b):
    return slice(8 * b, 8 * b + 8)


def residual_kernel(offs, nu_t, sg_t, p, src, ids, acc, nu, sg, fr, fc):
    first, last = row_masks()
    strip, tm = lax.axis_index("space"), lax.axis_index("tm")
    blocks = ROWS // 8
    for b in range(blocks):
        region = ids[rows8(b), :]
        nu[rows8(b), :] = lookup(region, nu_t)
        sg[rows8(b), :] = lookup(region, sg_t)
    for b in range(blocks):
        cur = nu[rows8(b), :]
        after = nu[rows8(min(b + 1, blocks - 1)), :]
        face = harmonic(cur, below(cur, after, last))
        if b == blocks - 1:
            face = jnp.where(last, 0.0, face)
        fr[rows8(b), :] = face
        fc[rows8(b), :] = harmonic(cur, pltpu.roll(cur, COLS - 1, 1))
    scale = signed() / (STEPS * lax.axis_size("tm"))
    acc[...] = jnp.zeros_like(acc)

    @pl.loop(0, STEPS)
    def _(k):
        own = jnp.where(strip < lax.axis_size("space") // 2, offs[k] * SLOT_W, 0)
        back = (-own) & (COLS - 1)

        def use(b, _, image):
            part = src[k, rows8(b), :] - pltpu.roll(image, own, 1)
            acc[rows8(b), :] += scale * part

        stencil(
            lambda b: pltpu.roll(p[k, rows8(b), :], back, 1),
            blocks,
            lambda b: fr[rows8(b), :],
            lambda b: sg[rows8(b), :],
            lambda b: fc[rows8(b), :],
            use,
        )


def residual(offs, nu_t, sg_t, p, src, ids):
    return pl.pallas_call(
        residual_kernel,
        in_specs=[SMEM] * 3 + [VMEM] * 3,
        out_specs=VMEM,
        out_shape=struct(ROWS, COLS),
        scratch_shapes=[pltpu.VMEM((ROWS, COLS), jnp.float32)] * 4,
        compiler_params=LIMIT,
        cost_estimate=pl.CostEstimate(flops=10_000_000, bytes_accessed=20_000_000, transcendentals=0),
    )(offs, nu_t, sg_t, p, src, ids)


def sides_kernel(offs, nu_t, acc, own_first, own_last, top, bot, mine, send):
    strip, tm = lax.axis_index("space"), lax.axis_index("tm")
    half_strips = lax.axis_size("space") // 2
    scale = signed() / (STEPS * lax.axis_size("tm"))
    core, y = tm & 1, (tm >> 1) & 1
    flip = core * 8 + y * 4
    rows = lax.broadcasted_iota(jnp.int32, (8, COLS), 0)
    parts = []
    for own, halo, kind, own_row, halo_row in (
        (own_first, top, strip - 1, 0, 7),
        (own_last, bot, strip + 1, 7, 0),
    ):
        inner = lookup(own[8:16, :], nu_t)[own_row : own_row + 1, :]
        outer = lookup(halo[8:16, :], nu_t)[halo_row : halo_row + 1, :]
        inner = jnp.broadcast_to(inner, (8, COLS))
        outer = jnp.broadcast_to(outer, (8, COLS))
        total = jnp.zeros((8, COLS), jnp.float32)
        for k in range(STEPS):
            turn = offs[k] * SLOT_W
            a = pltpu.roll(inner, jnp.where(strip < half_strips, turn, 0), 1)
            b = pltpu.roll(outer, jnp.where(kind < half_strips, turn, 0), 1)
            gap = own[k : k + 1, :] - halo[k : k + 1, :]
            total = total + harmonic(a, b) * jnp.broadcast_to(gap, (8, COLS))
        parts.append(jnp.where(rows == own_row, scale * total, 0.0))
    for out, shift in ((mine, 0), (send, 8)):
        for i in range(8):
            b = (i + shift) ^ flip
            edge = jnp.where(b == 0, 1.0, 0.0) * parts[0]
            edge = edge + jnp.where(b == ROWS // 8 - 1, 1.0, 0.0) * parts[1]
            out[rows8(i), :] = acc[block(b), :] - edge


def sides(offs, nu_t, acc, own_first, own_last, top, bot):
    return pl.pallas_call(
        sides_kernel,
        in_specs=[SMEM] * 2 + [VMEM] * 5,
        out_specs=[VMEM] * 2,
        out_shape=[struct(ROWS // 2, COLS)] * 2,
        compiler_params=LIMIT,
    )(offs, nu_t, acc, own_first, own_last, top, bot)


def operator_kernel(nu_t, sg_t, ids, top, bot, _, sg, fr, fc, dinv, nu):
    first, last = row_masks()
    strip = lax.axis_index("space")
    blocks = EXTENDED // 8
    for e in range(blocks):
        if e == 0:
            region = top[8:16, :].astype(jnp.int32)
        elif e == blocks - 1:
            region = bot[8:16, :].astype(jnp.int32)
        else:
            region = ids[rows8(e - 1), :]
        nu[rows8(e), :] = lookup(region, nu_t)
        sg[rows8(e), :] = lookup(region, sg_t)
    up = jnp.zeros((8, COLS), jnp.float32)
    for e in range(blocks):
        cur = nu[rows8(e), :]
        face = harmonic(cur, below(cur, nu[rows8(min(e + 1, blocks - 1)), :], last))
        fr[rows8(e), :] = face
        side = harmonic(cur, pltpu.roll(cur, COLS - 1, 1))
        fc[rows8(e), :] = side
        diagonal = sg[rows8(e), :] + above(face, up, first) + face + pltpu.roll(side, 1, 1) + side
        inverse = 1.0 / diagonal
        if e == 0:
            inverse = jnp.where(strip == 0, 0.0, inverse)
        if e == blocks - 1:
            inverse = jnp.where(strip == lax.axis_size("space") - 1, 0.0, inverse)
        dinv[rows8(e), :] = inverse
        up = face


def operator(nu_t, sg_t, ids, top, bot, after):
    return pl.pallas_call(
        operator_kernel,
        in_specs=[SMEM] * 2 + [VMEM] * 3 + [ANY],
        out_specs=[VMEM] * 4,
        out_shape=[struct(EXTENDED, COLS)] * 4,
        scratch_shapes=[pltpu.VMEM((EXTENDED, COLS), jnp.float32)],
        compiler_params=LIMIT,
    )(nu_t, sg_t, ids, top, bot, after)


def swap(x, bit):
    return lax.ppermute(x, "tm", [(i, i ^ bit) for i in range(lax.axis_size("tm"))])


def add_kernel(a, b, mine, send):
    n = mine.shape[0]
    mine[...] = a[:n, :] + b[:n, :]
    send[...] = a[n:, :] + b[n:, :]


def halves(a, b):
    n = a.shape[0] // 2
    return pl.pallas_call(
        add_kernel,
        in_specs=[VMEM] * 2,
        out_specs=[VMEM] * 2,
        out_shape=[struct(n, COLS)] * 2,
        compiler_params=LIMIT,
    )(a, b)


def merge_kernel(a, b, _, out):
    for z in range(out.shape[0]):
        piece = slice(z * 128, z * 128 + 128)
        out[z] = a[:, piece] + b[:, piece]


def merge(a, b, after, count):
    return pl.pallas_call(
        merge_kernel,
        in_specs=[VMEM, VMEM, ANY],
        out_specs=VMEM,
        out_shape=struct(count, a.shape[0], COLS // count),
        compiler_params=LIMIT,
    )(a, b, after)


def total_kernel(parts, out):
    total = parts[0]
    for i in range(1, parts.shape[0]):
        total = total + parts[i]
    for i in range(parts.shape[0]):
        out[i] = total


def total_for_all(parts):
    return pl.pallas_call(
        total_kernel,
        in_specs=[VMEM],
        out_specs=VMEM,
        out_shape=struct(*parts.shape),
        compiler_params=LIMIT,
    )(parts)


def among_z(blocks):
    groups = [[z * 4 + q for z in range(blocks.shape[0])] for q in range(4)]
    return lax.all_to_all(blocks, "tm", 0, 0, axis_index_groups=groups)


def gate_kernel(*_):
    pass


def gate(value, *after):
    return pl.pallas_call(
        gate_kernel,
        in_specs=[ANY] * (1 + len(after)),
        out_specs=ANY,
        out_shape=struct(*value.shape),
        input_output_aliases={0: 0},
        compiler_params=LIMIT,
    )(value, *after)


def edge_kernel(x, out):
    tm = lax.axis_index("tm")
    start = pl.multiple_of(jnp.where((tm & 3) == 0, 0, x.shape[1] - 8), 8)
    out[...] = x[:, pl.ds(start, 8), :]


def edge_rows(x):
    return pl.pallas_call(
        edge_kernel,
        in_specs=[VMEM],
        out_specs=VMEM,
        out_shape=struct(x.shape[0], 8, 128),
        compiler_params=LIMIT,
    )(x)


def for_core_kernel(x, other, edge_a, edge_b, out):
    quarter = x.shape[1]
    out[:, :quarter, :] = x[...]
    out[:, quarter : 2 * quarter, :] = other[...]
    out[:, 2 * quarter :, :] = edge_a[...] + edge_b[...]


def for_core(x, other, edge_a, edge_b):
    return pl.pallas_call(
        for_core_kernel,
        in_specs=[VMEM] * 4,
        out_specs=VMEM,
        out_shape=struct(x.shape[0], 2 * x.shape[1] + 8, 128),
        compiler_params=LIMIT,
    )(x, other, edge_a, edge_b)


def edge_routes(moments, strips):
    routes = []
    for flip in (0, 2):
        route = []
        for z in range(moments // 4):
            for s in range(strips):
                if s > 0:
                    route.append(((z * 4) * strips + s, (z * 4 + 1 + flip) * strips + s - 1))
                if s + 1 < strips:
                    route.append(((z * 4 + 3) * strips + s, (z * 4 + flip) * strips + s + 1))
        routes.append(route)
    return routes


def chebyshev_kernel(own, partner, sg, fr, fc, dinv, c_out, sums, target, res, s0, s1, c):
    tm = lax.axis_index("tm")
    core, y = tm & 1, (tm >> 1) & 1
    flip = core * 8 + y * 4
    blocks = EXTENDED // 8
    for ref, start in ((own, 0), (partner, 8)):
        for z in range(own.shape[0]):
            piece = slice(z * 128, z * 128 + 128)
            for i in range(8):
                target[block(((start + i) ^ flip) + 1), piece] = ref[z, rows8(i), :]
            halo = ref[z, 64:72, :]
            at = jnp.where(core == start // 8, 0, blocks - 1)
            target[block(at), piece] = halo

    center = (MAXIMUM + MINIMUM) / 2.0
    half_span = (MAXIMUM - MINIMUM) / 2.0
    ratio = center / half_span
    for e in range(blocks):
        step = target[rows8(e), :] * dinv[rows8(e), :] / center
        s0[rows8(e), :] = step
        c[rows8(e), :] = step

    def sweep(field, use):
        stencil(
            lambda e: field[rows8(e), :],
            blocks,
            lambda e: fr[rows8(e), :],
            lambda e: sg[rows8(e), :],
            lambda e: fc[rows8(e), :],
            use,
        )

    old = 1.0 / ratio
    now, then = s0, s1
    for number in range(SWEEPS - 1):
        new = 1.0 / (2.0 * ratio - old)

        def use(e, cur, image):
            left = (target if number == 0 else res)[rows8(e), :] - image
            res[rows8(e), :] = left
            step = new * old * cur + (2.0 * new / half_span) * (left * dinv[rows8(e), :])
            then[rows8(e), :] = step
            c[rows8(e), :] += step

        sweep(now, use)
        now, then = then, now
        old = new

    totals = [jnp.zeros((8, COLS), jnp.float32)] * 2

    def finish(e, cur, image):
        if 0 < e < blocks - 1:
            c_out[rows8(e - 1), :] = cur
            totals[0] = totals[0] + target[rows8(e), :] * cur
            totals[1] = totals[1] + cur * image

    sweep(c, finish)
    sums[...] = jnp.zeros_like(sums)
    for i in range(2):
        sums[:, i : i + 1, :] = jnp.full((sums.shape[0], 1, 128), jnp.sum(totals[i]), jnp.float32)


def chebyshev(own, partner, sg, fr, fc, dinv, strips):
    return pl.pallas_call(
        chebyshev_kernel,
        in_specs=[VMEM] * 6,
        out_specs=[VMEM] * 2,
        out_shape=[struct(ROWS, COLS), struct(strips, 8, 128)],
        scratch_shapes=[pltpu.VMEM((EXTENDED, COLS), jnp.float32)] * 5,
        compiler_params=LIMIT,
        cost_estimate=pl.CostEstimate(flops=10_000_000, bytes_accessed=10_000_000, transcendentals=0),
    )(own, partner, sg, fr, fc, dinv)


def step_length(sums):
    every = sums[0]
    for i in range(1, sums.shape[0]):
        every = every + sums[i]
    return jnp.sum(every[0:1, 0:1]) / jnp.sum(every[1:2, 0:1])


def signed():
    tm = lax.axis_index("tm")
    return jnp.where(tm < lax.axis_size("tm") // 2, 1.0, -1.0).astype(jnp.float32)


def update_kernel(starts, fresh, *refs):
    refs = refs if fresh else refs[1:]
    sums, c, p = refs[:3]
    opposite, refs = refs[3 : 3 + len(starts)], refs[3 + len(starts) :]
    if fresh:
        out, correction, buffer, kept, out_sem, kept_sem = refs
    else:
        out, buffer, out_sem = refs
    omega, sign = step_length(sums), signed()
    copies = []
    for i, (start, part) in enumerate(zip(starts, opposite)):
        for r in range(0, part.shape[1], 8):
            here = slice(start + r, start + r + 8)
            corrected = omega * c[here, :]
            for k in range(STEPS):
                field = p[k, here, :]
                moved = field - 0.5 * (field + part[k, r : r + 8, :])
                buffer[k, here, :] = moved + sign * corrected
        rows = pl.ds(start, part.shape[1])
        copies.append(pltpu.make_async_copy(buffer.at[:, rows], out.at[:, rows], out_sem.at[i]))
        copies[-1].start()
    if fresh:
        kept[...] = omega * c[...]
        copies.append(pltpu.make_async_copy(kept, correction, kept_sem))
        copies[-1].start()
    for copy in copies:
        copy.wait()


def update(done, sums, c, p, opposite, starts):
    fresh = done is None
    shape, strip = (STEPS, ROWS, COLS), (ROWS, COLS)
    sems = pltpu.SemaphoreType.DMA((len(starts),))
    buffer = pltpu.VMEM(shape, jnp.float32)
    operands = (sums, c, p, *opposite)
    return pl.pallas_call(
        functools.partial(update_kernel, starts, fresh),
        in_specs=([] if fresh else [ANY]) + [VMEM] * len(operands),
        out_specs=[ANY] * 2 if fresh else ANY,
        out_shape=[struct(*shape), struct(*strip)] if fresh else struct(*shape),
        scratch_shapes=(
            [buffer, pltpu.VMEM(strip, jnp.float32), sems, pltpu.SemaphoreType.DMA]
            if fresh
            else [buffer, sems]
        ),
        input_output_aliases={} if fresh else {0: 0},
        compiler_params=LIMIT,
    )(*(operands if fresh else (done,) + operands))


def per_device(p, source, offsets, ids, nu_t, sg_t):
    moments = lax.axis_size("tm")
    strips = lax.axis_size("space")
    across = [(i, (i + moments // 2) % moments) for i in range(moments)]
    to_next = [(i, i + 1) for i in range(strips - 1)]
    to_prev = [(j, i) for i, j in to_next]
    starts = [sum(CHUNKS[:i]) for i in range(len(CHUNKS))]

    def ready(i, *after):
        rows = lax.slice_in_dim(p, starts[i], starts[i] + CHUNKS[i], axis=1)
        return lax.ppermute(gate(rows, *after), "tm", across)

    opposite = [lax.ppermute(p[:, : CHUNKS[0]], "tm", across)]
    down, up = edges(p, ids)
    top = lax.ppermute(up, "space", to_next)
    bot = lax.ppermute(down, "space", to_prev)
    acc = residual(offsets, nu_t, sg_t, p, source, ids)
    mine, send = sides(offsets, nu_t, acc, down, up, top, bot)

    mine, send = halves(mine, swap(send, 1))
    pieces = merge(mine, swap(send, 2), opposite[0], moments // 4)
    opposite.append(ready(1, pieces))
    total = total_for_all(among_z(pieces))
    opposite.append(ready(2, opposite[1]))
    x = among_z(total)
    opposite.append(ready(3, x, opposite[2]))
    sg, fr, fc, dinv = operator(nu_t, sg_t, ids, top, bot, x)
    opposite.append(ready(4, sg))

    edge = edge_rows(x)
    edge_a, edge_b = (lax.ppermute(edge, ("tm", "space"), r) for r in edge_routes(moments, strips))
    own = for_core(x, swap(x, 2), edge_a, edge_b)
    c, sums = chebyshev(own, swap(own, 1), sg, fr, fc, dinv, strips)
    sums = lax.all_to_all(sums, "space", 0, 0)
    updated, correction = update(None, sums, c, p, opposite[:-1], starts[:-1])
    return update(updated, sums, c, p, opposite[-1:], starts[-1:]), correction


def solution(mesh):
    placed = (P("tm", "space", None), P("tm", "space", None), P("tm"), P("space", None), P(), P())
    return jax.shard_map(
        per_device,
        mesh=mesh,
        in_specs=placed,
        out_specs=(P("tm", "space", None), P("space", None)),
        check_vma=False,
    )
```
